128 devices in a mesh: fsdp: 4 (over z), dp: 4 (over y_hi, core), outer: 8 (over x, y_lo).
Axes of the slice: x: 4, y: 4 (y_hi: 2, y_lo: 2; y = y_hi * 2 + y_lo), z: 4, core: 2. Of those that a mesh axis runs over, the one named last changes fastest.
Arguments:
- grad_parts: bfloat16 [8, 4, 4, 8192, 512], P('outer', 'fsdp', 'dp'), may hold values from -6 to 6
- momentum: float32 [8, 8192, 512], P('outer', ('fsdp', 'dp')), may hold values from -6 to 6
- params: float32 [8192, 512], P(('fsdp', 'dp')), may hold values from -6 to 6
- band: int32 [256], replicated, may hold values from 0 to 4095, as said below
Outputs:
- new_momentum: float32 [8, 8192, 512], P('outer', ('fsdp', 'dp'))
- new_params: float32 [8192, 512], P('fsdp')
The draws below stay inside these ranges and needn't reach their ends.
Inputs may be any that keep to these rules, and one draw needn't show every extreme that they name: `band`: 256 distinct positions, each vertical frequency times 64 plus horizontal frequency.
All inputs are finite; a program needn't handle non-finite values.
Results may differ from the reference program's by a relative error of at most 0.0003.
Values sent between devices are 32-bit elements; how exact they have to be, the bound alone decides.
No kernel may reach another device: no remote copies, remote signals or barrier semaphores. Data moves between devices by JAX's collectives and lax.ppermute only.
A program may use at most 192 MiB of HBM per device.

```python
import jax
import jax.numpy as jnp
from jax import lax

ROWS = 8192
COLS = 512
GROUP = 64
BAND = 256
N_FSDP = 4
N_DP = 4
N_OUTER = 8


def draw_band(key, part):
    key = jax.random.fold_in(key, 7)
    order = jax.random.permutation(key, GROUP * GROUP - 2) + 1
    first = jnp.zeros((1,), jnp.int32)
    last = jnp.full((1,), GROUP * GROUP - 1, jnp.int32)
    return jnp.concatenate([first, order[:BAND - 2].astype(jnp.int32), last]).astype(jnp.int32)


def block_scale(own_key, extent, cuts, low, top_value):
    def one(position, blocks):
        steps = jax.random.uniform(jax.random.fold_in(jax.random.fold_in(own_key, 6), position), (blocks,), jnp.float32, low / len(cuts), top_value / len(cuts))
        return jnp.repeat(jnp.exp(steps), extent[position] // blocks).reshape((-1,) + (1,) * (len(extent) - position - 1))

    factor_of = one(*cuts[0])
    for cut in cuts[1:]:
        factor_of = factor_of * one(*cut)
    return factor_of


def centred(own_key, shape, spread, bound, shards=(), held_as=jnp.bfloat16):
    result = spread * jax.random.normal(own_key, shape, jnp.float32)
    if shards:
        result = result * block_scale(own_key, shape, shards, -0.22, 0.18)
    return jnp.clip(result, -bound, bound).astype(held_as)


def setup_inputs(seed: int = 0) -> dict:
    seeds = jax.random.split(jax.random.key(seed), 5)
    grad_parts = centred(seeds[0], (N_OUTER, N_FSDP, N_DP, ROWS, COLS), 1.0, 6.0, ((0, 8), (1, 4), (2, 4)))
    momentum = centred(seeds[1], (N_OUTER, ROWS, COLS), 1.0, 6.0, ((0, 8), (1, 16)), jnp.float32)
    params = centred(seeds[2], (ROWS, COLS), 1.0, 6.0, ((0, 16),), jnp.float32)
    band = draw_band(jax.random.fold_in(seeds[4], 71), 0)
    return dict(grad_parts=grad_parts, momentum=momentum, params=params, band=band)


beta = 0.9

def dct_table():
    freq = jnp.arange(GROUP, dtype=jnp.float32)[:, None]
    place = jnp.arange(GROUP, dtype=jnp.float32)[None, :]
    scale = jnp.where(freq == 0, jnp.sqrt(1.0 / GROUP), jnp.sqrt(2.0 / GROUP)).astype(jnp.float32)
    return (scale * jnp.cos(jnp.pi * (2.0 * place + 1.0) * freq / (2.0 * GROUP))).astype(jnp.float32)

def encode(field, table):
    rows, cols = field.shape
    blocks = field.reshape(rows // GROUP, GROUP, cols // GROUP, GROUP)
    half = jnp.einsum('km,ambn->akbn', table, blocks, precision=lax.Precision.HIGHEST)
    coeff = jnp.einsum('akbn,ln->abkl', half, table, precision=lax.Precision.HIGHEST)
    return coeff.reshape(rows // GROUP, cols // GROUP, GROUP * GROUP)

def decode(shared, band, table):
    nrow, ncol = (shared.shape[0], shared.shape[1])
    placed = jnp.zeros((nrow, ncol, GROUP * GROUP), jnp.float32).at[:, :, band].set(shared)
    placed = placed.reshape(nrow, ncol, GROUP, GROUP)
    half = jnp.einsum('km,abkl->ambl', table, placed, precision=lax.Precision.HIGHEST)
    field = jnp.einsum('ambl,ln->ambn', half, table, precision=lax.Precision.HIGHEST)
    return field.reshape(nrow * GROUP, ncol * GROUP)

def reference(grad_parts, momentum, params, band):
    table = dct_table()
    grad = lax.optimization_barrier(jnp.sum(grad_parts.astype(jnp.float32), axis=(1, 2))) * (1.0 / (N_FSDP * N_DP))
    mom = beta * momentum + grad
    new_momentum = []
    total = None
    for pod in range(N_OUTER):
        coeff = encode(mom[pod], table)
        shared = coeff[:, :, band]
        new_momentum.append(mom[pod] - decode(shared, band, table))
        total = shared if total is None else total + shared
    new_params = params - decode(total * (1.0 / N_OUTER), band, table)
    return (jnp.stack(new_momentum), new_params)
```

```python
import jax
import jax.numpy as jnp
from jax import lax
from jax.experimental import pallas as pl
from jax.experimental.pallas import tpu as pltpu
from jax.sharding import PartitionSpec as P

GROUP = 64
BAND = 256
COLS = 512
NB = COLS // GROUP
OWN = 512
AXES = ("fsdp", "dp", "outer")
beta = 0.9

F32 = jnp.float32
BF16 = jnp.bfloat16


def place(x, y, z, core):
    return z * 32 + ((y // 2) * 2 + core) * 8 + x * 2 + y % 2


def swap(value, x=0, y=0, z=0, core=0):
    pairs = []
    for px in range(4):
        for py in range(4):
            for pz in range(4):
                for pc in range(2):
                    pairs.append((place(px, py, pz, pc), place(px ^ x, py ^ y, (pz + z) % 4, pc ^ core)))
    return lax.ppermute(value, AXES, pairs)


def cosine_columns(freq):
    freq = freq.astype(F32)[None, :]
    pos = jnp.arange(GROUP, dtype=F32)[:, None]
    scale = jnp.where(freq == 0, jnp.sqrt(1.0 / GROUP), jnp.sqrt(2.0 / GROUP)).astype(F32)
    return scale * jnp.cos(jnp.pi * (2.0 * pos + 1.0) * freq / (2.0 * GROUP))


def split(value):
    high = value.astype(BF16)
    return high, (value - high.astype(F32)).astype(BF16)


def dot(a, b):
    return jnp.dot(a, b, preferred_element_type=F32)


def mom_kernel(grad_ref, momentum_ref, vert_ref, horiz_ref, mom_ref, shared_ref):
    rows = grad_ref.shape[0]
    mom = beta * momentum_ref[...] + grad_ref[...] * (1.0 / 16.0)
    mom_ref[...] = mom
    vert = vert_ref[...][None]
    w_high, w_low = split(horiz_ref[...])
    x_high, x_low = split(mom)
    for b in range(NB):
        cut = slice(b * GROUP, (b + 1) * GROUP)
        half = dot(x_high[:, cut], w_high) + dot(x_low[:, cut], w_high) + dot(x_high[:, cut], w_low)
        half = half.reshape(rows // GROUP, GROUP, BAND)
        shared_ref[:, b, :] = jnp.sum(half * vert, axis=1)


def take_out(field, coeff, vert, w_both):
    rows = field.shape[0]
    out = []
    for b in range(NB):
        wide = coeff[:, b, :][:, None, :] * vert[None]
        high, low = split(wide.reshape(rows, BAND))
        both = dot(high, w_both)
        out.append(both[:, :GROUP] + both[:, GROUP:] + dot(low, w_both[:, :GROUP]))
    return field - jnp.concatenate(out, axis=1)


def residual_kernel(mom_ref, shared_ref, vert_ref, horiz_t_ref, out_ref):
    high, low = split(horiz_t_ref[...])
    w_both = jnp.concatenate([high, low], axis=1)
    out_ref[...] = take_out(mom_ref[...], shared_ref[...], vert_ref[...], w_both)


def update_kernel(at_ref, params_ref, total_ref, vert_ref, horiz_t_ref, out_ref):
    high, low = split(horiz_t_ref[...])
    w_both = jnp.concatenate([high, low], axis=1)
    out_ref[...] = take_out(params_ref[...], total_ref[0] * (1.0 / 8.0), vert_ref[...], w_both)


def full(shape):
    return pl.BlockSpec(shape, lambda *_: (0,) * len(shape))


def mom_call(grad, momentum, vert, horiz):
    rows = 128
    return pl.pallas_call(
        mom_kernel,
        grid=(OWN // rows,),
        in_specs=[
            pl.BlockSpec((rows, COLS), lambda i: (i, 0)),
            pl.BlockSpec((rows, COLS), lambda i: (i, 0)),
            full((GROUP, BAND)),
            full((GROUP, BAND)),
        ],
        out_specs=[
            pl.BlockSpec((rows, COLS), lambda i: (i, 0)),
            pl.BlockSpec((rows // GROUP, NB, BAND), lambda i: (i, 0, 0)),
        ],
        out_shape=[
            jax.ShapeDtypeStruct((OWN, COLS), F32),
            jax.ShapeDtypeStruct((OWN // GROUP, NB, BAND), F32),
        ],
        name="momentum_encode",
    )(grad, momentum, vert, horiz)


def residual_call(mom, shared, vert, horiz_t):
    rows = 128
    return pl.pallas_call(
        residual_kernel,
        grid=(OWN // rows,),
        in_specs=[
            pl.BlockSpec((rows, COLS), lambda i: (i, 0)),
            pl.BlockSpec((rows // GROUP, NB, BAND), lambda i: (i, 0, 0)),
            full((GROUP, BAND)),
            full((BAND, GROUP)),
        ],
        out_specs=pl.BlockSpec((rows, COLS), lambda i: (i, 0)),
        out_shape=jax.ShapeDtypeStruct((OWN, COLS), F32),
        cost_estimate=pl.CostEstimate(flops=2 * 10**9, bytes_accessed=2 * 2**20, transcendentals=0),
        name="momentum_residual",
    )(mom, shared, vert, horiz_t)


def update_call(which, params, total, vert, horiz_t):
    rows = 256
    per = OWN // rows
    return pl.pallas_call(
        update_kernel,
        grid_spec=pltpu.PrefetchScalarGridSpec(
            num_scalar_prefetch=1,
            grid=(4, per),
            in_specs=[
                pl.BlockSpec((rows, COLS), lambda i, r, at: (i * per + r, 0)),
                pl.BlockSpec((1, rows // GROUP, NB, BAND), lambda i, r, at: (i, r, 0, 0)),
                full((GROUP, BAND)),
                full((BAND, GROUP)),
            ],
            out_specs=pl.BlockSpec((rows, COLS), lambda i, r, at: (at[i] * per + r, 0)),
        ),
        out_shape=jax.ShapeDtypeStruct((4 * OWN, COLS), F32),
        name="parameter_update",
    )(which, params, total, vert, horiz_t)


def local(grad_parts, momentum, params, band):
    dp = lax.axis_index("dp")
    band = band.astype(jnp.int32)
    vert = cosine_columns(band // GROUP)
    horiz = cosine_columns(band % GROUP)
    horiz_t = horiz.T

    partial_value = grad_parts.reshape(grad_parts.shape[3], grad_parts.shape[4]).astype(F32)
    summed = lax.psum_scatter(partial_value, ("fsdp", "dp"), scatter_dimension=0, tiled=True)

    far = swap(params, y=3)
    both = jnp.concatenate([params, far], axis=0)
    near = swap(both, core=1)
    every = jnp.concatenate([params, near[:OWN], far, near[OWN:]], axis=0)

    mom, shared = mom_call(summed, momentum[0], vert, horiz)
    new_momentum = residual_call(mom, shared, vert, horiz_t)

    total = (shared + swap(shared, x=1)) + (swap(shared, x=2) + swap(shared, x=3))
    here = total + swap(total, y=1)
    there = swap(total, y=2) + swap(total, y=3)
    pair = jnp.stack([here, there])
    other = swap(pair, core=1)
    totals = jnp.stack([pair[0], other[0], pair[1], other[1]])
    which = dp ^ jnp.arange(4, dtype=jnp.int32)
    new_params = update_call(which, every, totals, vert, horiz_t)
    return (new_momentum[None], new_params)


def solution(mesh):
    return jax.shard_map(
        local,
        mesh=mesh,
        in_specs=(
            P("outer", "fsdp", "dp", None, None),
            P("outer", ("fsdp", "dp"), None),
            P(("fsdp", "dp"), None),
            P(),
        ),
        out_specs=(P("outer", ("fsdp", "dp"), None), P("fsdp", None)),
        check_vma=False,
    )
```

```python
import jax
import jax.numpy as jnp
from jax import lax
from jax.experimental import pallas as pl
from jax.experimental.pallas import tpu as pltpu
from jax.sharding import PartitionSpec as P

GROUP = 64
BAND = 256
COLS = 512
NB = COLS // GROUP
OWN = 512
ZROWS = 320
LANES = COLS // 128
AXES = ("fsdp", "dp", "outer")
beta = 0.9

F32 = jnp.float32
BF16 = jnp.bfloat16


def place(x, y, z, core):
    return z * 32 + ((y // 2) * 2 + core) * 8 + x * 2 + y % 2


def swap(value, x=0, y=0, z=0, core=0):
    pairs = []
    for px in range(4):
        for py in range(4):
            for pz in range(4):
                for pc in range(2):
                    pairs.append((place(px, py, pz, pc), place(px ^ x, py ^ y, (pz + z) % 4, pc ^ core)))
    return lax.ppermute(value, AXES, pairs)


def cosine_columns(freq):
    freq = freq.astype(F32)[None, :]
    pos = jnp.arange(GROUP, dtype=F32)[:, None]
    scale = jnp.where(freq == 0, jnp.sqrt(1.0 / GROUP), jnp.sqrt(2.0 / GROUP)).astype(F32)
    return scale * jnp.cos(jnp.pi * (2.0 * pos + 1.0) * freq / (2.0 * GROUP))


def split(value):
    high = value.astype(BF16)
    return high, (value - high.astype(F32)).astype(BF16)


def dot(a, b):
    return jnp.dot(a, b, preferred_element_type=F32)


def piece_shape(step):
    f, _, _, _, rows = step
    return (2, rows, COLS) if isinstance(f, str) else (rows, COLS)


def piece_source(step, z, yh, core, parts_ref):
    f, r, c, top, rows = step
    cut = pl.ds(top, rows)
    r_at, c_at = (yh + r) % 2, (core + c) % 2
    if isinstance(f, str):
        lo = (z + (1 if f == "sides" else 0)) % 2
        return parts_ref.at[:, lo, r_at, c_at, cut, :]
    to = (z + f) % 4
    return parts_ref.at[to // 2, to % 2, r_at, c_at, cut, :]


def mark(z, piece, term, out):
    out[...] = jnp.zeros((8, 128), F32)


def piece_call(name, parts, steps, terms, after, outs, cost=1):
    outs = outs + [((8, 128), mark)]
    outs = [out if len(out) == 3 else out + (F32,) for out in outs]
    terms = [t if isinstance(t, tuple) else (t, t.shape, lambda x, ref: ref) for t in terms]
    n_terms, n_after, n_outs, n_steps = len(terms), len(after), len(outs), len(steps)

    def kernel(parts_ref, *refs):
        refs = list(refs)
        take = lambda n: [refs.pop(0) for _ in range(n)]
        term_refs, _, out_refs = take(n_terms), take(n_after), take(n_outs)
        bufs, held, built = take(n_steps), take(n_terms), take(n_outs)
        load_sems, out_sems = take(n_steps + n_terms), take(n_outs)
        z, dp, x = lax.axis_index("fsdp"), lax.axis_index("dp"), lax.axis_index("outer") // 2
        sources = [piece_source(s, z, dp // 2, dp % 2, parts_ref) for s in steps]
        sources += [pick(x, ref) for (_, _, pick), ref in zip(terms, term_refs)]
        loads = []
        for src, buf, sem in zip(sources, bufs + held, load_sems):
            copy = pltpu.make_async_copy(src, buf, sem)
            copy.start()
            loads.append(copy)
        waiting = set(range(len(loads)))

        def loaded(i):
            if i in waiting:
                waiting.remove(i)
                loads[i].wait()
            return (bufs + held)[i]

        stores = []
        for (_, body, _), ref, buf, sem in zip(outs, out_refs, built, out_sems):
            body(z, loaded, lambda i: loaded(n_steps + i), buf)
            copy = pltpu.make_async_copy(buf, ref, sem)
            copy.start()
            stores.append(copy)
        for i in sorted(waiting):
            loads[i].wait()
        for copy in stores:
            copy.wait()

    anywhere = pl.BlockSpec(memory_space=pl.ANY)
    return pl.pallas_call(
        kernel,
        in_specs=[pl.BlockSpec(memory_space=pltpu.HBM)] + [anywhere] * (n_terms + n_after),
        out_specs=[anywhere] * n_outs,
        out_shape=[jax.ShapeDtypeStruct(s, t) for s, _, t in outs],
        scratch_shapes=[pltpu.VMEM(piece_shape(s), BF16) for s in steps]
        + [pltpu.VMEM(s, F32) for _, s, _ in terms]
        + [pltpu.VMEM(s, t) for s, _, t in outs]
        + [pltpu.SemaphoreType.DMA] * (n_steps + n_terms + n_outs),
        compiler_params=pltpu.CompilerParams(vmem_limit_bytes=40 * 2**20),
        cost_estimate=pl.CostEstimate(flops=1, bytes_accessed=cost, transcendentals=0),
        name=name,
    )(parts, *[t for t, _, _ in terms], *after)


def encode(mom, vert, horiz):
    rows = mom.shape[0]
    w_high, w_low = split(horiz)
    x_high, x_low = split(mom)
    out = []
    for b in range(NB):
        cut = slice(b * GROUP, (b + 1) * GROUP)
        half = dot(x_high[:, cut], w_high) + dot(x_low[:, cut], w_high) + dot(x_high[:, cut], w_low)
        out.append(jnp.sum(half.reshape(rows // GROUP, GROUP, BAND) * vert[None], axis=1))
    return out


def step_rows(grad_parts, momentum, params, vert, horiz):
    parts = pltpu.with_memory_space_constraint(grad_parts.reshape(2, 2, 2, 2, OWN, COLS), pltpu.HBM)
    vert_t, horiz_t = vert.T, horiz.T
    zr, yr, half = ZROWS, OWN - ZROWS, COLS // 2
    zs, ys = (zr, COLS), (yr, COLS)
    zh, yhs = (zr, half), (yr, half)
    left, right = slice(0, half), slice(half, COLS)
    call = lambda name, *rest, **options: piece_call(name, parts, *rest, **options)

    def widen(name, groups, after):
        outs, first = [], 0
        for group in groups:
            counts = [2 * s[4] if isinstance(s[0], str) else s[4] for s in group]

            def body(z, piece, term, out, counts=counts, first=first):
                top = 0
                for i, n in enumerate(counts):
                    out[top:top + n, :] = piece(first + i)[...].reshape(n, COLS).astype(F32)
                    top += n

            outs.append(((sum(counts), COLS), body))
            first += len(group)
        return call(name, [s for group in groups for s in group], [], after, outs)

    def rows_of(ref, top, n, cols=slice(None)):
        return ref[top:top + n, cols]

    def side(ref, top, n, at_f, cols):
        return ref[pl.ds(pl.multiple_of(top + at_f * n, 64), n), cols]

    def hi(z, f):
        return ((z + f) % 4) // 2

    def halves(top):
        def body(cols):
            def run(z, piece, term, out):
                out[...] = rows_of(term(0), top, zr, cols) + piece(0)[:, cols].astype(F32)
            return run
        return [(zh, body(left)), (zh, body(right))]

    quarter = OWN // 4
    far_rows, crossed_rows = 2 * yr, 2 * yr + quarter

    def crossing(i_piece, i_term, top, i_params):
        def run(z, piece, term, out):
            for h in range(2):
                out[h * yr:(h + 1) * yr, :] = rows_of(term(i_term), top + h * yr, yr) + piece(i_piece)[h].astype(F32)
            out[far_rows:, :] = term(i_params)[...]
        return run

    def params_quarter(i):
        def pick(x, ref):
            return ref.at[pl.ds(pl.multiple_of((x % 2) * (2 * quarter) + i * quarter, quarter), quarter), :]
        return (params, (quarter, COLS), pick)

    def sides(i_piece, got, i_add):
        def body(f, h_add, i_add):
            def run(z, piece, term, out):
                k = hi(z, f)
                for h, cols in enumerate((left, right)):
                    value = got(term, f, k, cols) + piece(i_piece)[k, :, cols].astype(F32)
                    out[:, cols] = value + term(i_add)[...] if h == h_add else value
            return run
        return [(zs, body(1, 0, i_add)), (zs, body(3, 1, i_add + 1))]

    up, down = (lambda v: swap(v, z=1)), (lambda v: swap(v, z=3))
    wa, ta = widen("widen_a", [[(2, 1, 1, 0, zr), ("even", 1, 1, zr, yr)]], [])
    ca = swap(wa, core=1)
    wb, tb = widen("widen_b", [[("sides", 1, 1, 0, zr), (2, 0, 1, 0, zr)]], [ta])
    cb = swap(wb, core=1)
    u1, d1, y1, t1 = call("far_opposite", [(2, 1, 0, 0, zr), ("even", 1, 0, zr, yr)], [ca, params_quarter(0)], [tb],
                          halves(0) + [((crossed_rows, COLS), crossing(1, 0, zr, 1))])
    gu1, gd1, gy1 = up(u1), down(d1), swap(y1, y=2)
    *wc, tc = widen("widen_c", [[("sides", 1, 1, zr, yr)], [("even", 0, 1, zr, yr)]], [t1])
    c_cross, c_last = [swap(w, core=1) for w in wc]
    u2, d2, t2 = call("near_opposite", [(2, 0, 0, 0, zr)], [cb], [tc], halves(2 * zr))
    gu2, gd2 = up(u2), down(d2)
    u3, d3, y2, t3 = call("far_sides", [("sides", 1, 0, 0, zr), ("sides", 1, 0, zr, yr)],
                          [cb, gu1, gd1, c_cross, params_quarter(1)], [t2],
                          sides(0, lambda term, f, k, cols: side(term(0), 0, zr, k, cols), 1)
                          + [((crossed_rows, COLS), crossing(1, 3, 0, 4))])
    gu3, gd3, gy2 = up(u3), down(d3), swap(y2, y=2)
    *wd, td = widen("widen_d", [[(1, 0, 1, 0, zr)], [(3, 0, 1, 0, zr)], [(0, 1, 1, 0, zr)], [(0, 0, 1, 0, zr)],
                                [("sides", 0, 1, zr, yr)]], [t3, gu2, gd2])
    c_up, c_down, c_far, c_near, c_sides = [swap(w, core=1) for w in wd]
    table_high, table_low, tt = call("band_table", [], [vert_t, horiz_t], [td], band_table())

    def last_half(cols):
        def run(z, piece, term, out):
            k = hi(z, 2)
            out[...] = side(term(0), 0, yr, k, cols) + side(term(1), 0, yr, k, cols) + piece(0)[k, :, cols].astype(F32)
        return run

    def last_own_body(z, piece, term, out):
        k = z // 2
        out[...] = side(term(0), 0, yr, k, slice(None)) + side(term(1), 0, yr, k, slice(None)) + piece(0)[k].astype(F32)

    u4, d4, last_own, t4 = call("last_opposite", [("even", 0, 0, zr, yr)], [gy1, c_last], [tt],
                            [(yhs, last_half(left)), (yhs, last_half(right)), (ys, last_own_body)])
    gu4, gd4 = up(u4), down(d4)
    u5, d5, t5 = call("near_sides", [("sides", 0, 0, 0, zr)], [c_up, c_down, gu2, gd2], [t4, gu3, gd3],
                      sides(0, lambda term, f, k, cols: term(0 if f == 1 else 1)[:, cols], 2))
    gu5, gd5 = up(u5), down(d5)

    def cross_body(z, piece, term, out):
        out[...] = term(0)[...] + piece(0)[...].astype(F32) + (term(1)[...] + term(2)[...])

    y3, tx = call("far_cross", [(0, 1, 0, 0, zr)], [c_far, gu3, gd3], [t5], [(zs, cross_body)])
    gy3 = swap(y3, y=2)

    def last_sides(f, h_add, i_add):
        def run(z, piece, term, out):
            k = hi(z, f)
            for h, cols in enumerate((left, right)):
                value = side(term(0), 0, yr, k, cols) + side(term(1), 0, yr, k, cols) + piece(0)[k, :, cols].astype(F32)
                out[:, cols] = value + term(i_add)[...] if h == h_add else value
        return run

    def half_body(z, piece, term, out):
        out[:quarter, :] = term(4)[...]
        out[quarter:, :] = term(0)[far_rows:, :]

    last_quarter = (gy1, (quarter, COLS), lambda x, ref: ref.at[pl.ds(far_rows, quarter), :])
    u6, d6, far_half, t6 = call("last_sides", [("sides", 0, 0, zr, yr)], [gy2, c_sides, gu4, gd4, last_quarter], [tx],
                            [(ys, last_sides(1, 0, 2)), (ys, last_sides(3, 1, 3)), ((2 * quarter, COLS), half_body)])
    gu6, gd6 = up(u6), down(d6)

    def momentum_rows(top, n):
        return (momentum, (n, COLS), lambda x, ref: ref.at[pl.ds(top, n), :])

    def near_mom(z, piece, term, out):
        mine = term(0)[...] + piece(0)[...].astype(F32)
        grad = mine + (term(1)[...] + term(2)[...]) + term(3)[...]
        out[...] = beta * term(4)[...] + grad * (1.0 / 16.0)
        near_mom.value = out

    def near_shared(z, piece, term, out):
        for b, value in enumerate(encode(near_mom.value[...], term(5)[...], term(6)[...])):
            out[b] = value

    nz, ny = zr // GROUP, yr // GROUP
    mom_top, shared_top, t7 = call(
        "near_momentum", [(0, 0, 0, 0, zr)], [c_near, gu5, gd5, gy3, momentum_rows(0, zr), vert, horiz], [t6],
        [(zs, near_mom), ((NB, nz, BAND), near_shared)], cost=9 * 10**6,
    )

    def last_mom(z, piece, term, out):
        grad = term(0)[...] + (term(1)[...] + term(2)[...])
        out[...] = beta * term(3)[...] + grad * (1.0 / 16.0)
        last_mom.value = out

    def last_shared(z, piece, term, out):
        for b, value in enumerate(encode(last_mom.value[...], term(4)[...], term(5)[...])):
            out[b, :nz, :] = term(6)[b]
            out[b, nz:, :] = value

    mom_low, shared, t8 = call(
        "last_momentum", [], [last_own, gu6, gd6, momentum_rows(zr, yr), vert, horiz, shared_top], [t7],
        [(ys, last_mom), ((NB, nz + ny, BAND), last_shared)],
    )

    def pack(z, piece, term, out):
        out[:OWN, :] = term(0)[...]
        out[OWN:, :] = term(1)[...]

    packed, _ = call("params_pack", [], [params, far_half], [t6], [((OWN + 2 * quarter, COLS), pack)])

    def residual(z, piece, term, out):
        high, low = split(term(4)[...])
        w_both = jnp.concatenate([high, low], axis=1)
        vert_now = term(3)[...][None]
        for pair in range(NB // 2):
            sides = []
            for b in (2 * pair, 2 * pair + 1):
                wide = (term(2)[b][:, None, :] * vert_now).reshape(OWN, BAND)
                wide_high, wide_low = split(wide)
                both = dot(wide_high, w_both)
                sides.append(both[:, :GROUP] + both[:, GROUP:] + dot(wide_low, w_both[:, :GROUP]))
            cols = slice(pair * 2 * GROUP, (pair + 1) * 2 * GROUP)
            value = jnp.concatenate(sides, axis=1)
            out[:zr, cols] = term(0)[:, cols] - value[:zr]
            out[zr:, cols] = term(1)[:, cols] - value[zr:]

    new_momentum, t9 = call("momentum_residual", [], [mom_top, mom_low, shared, vert, horiz_t], [t8],
                            [((OWN, COLS), residual)], cost=9 * 10**6)

    def sum_four(z, piece, term, out):
        out[...] = (term(0)[...] + term(1)[...]) + (term(2)[...] + term(3)[...])

    def sum_pairs(z, piece, term, out):
        out[0] = term(0)[...] + term(1)[...]
        out[1] = term(2)[...] + term(3)[...]

    total, t10 = call("sum_x", [], [shared] + [swap(shared, x=k) for k in (1, 2, 3)], [t9], [(shared.shape, sum_four)])
    pair, _ = call("sum_y", [], [total] + [swap(total, y=k) for k in (1, 2, 3)], [], [((2,) + shared.shape, sum_pairs)])
    far_other = swap(far_half, x=1)
    new_params = update_call(params, swap(packed, core=1), far_half, far_other, swap(far_other, core=1),
                             pair, swap(pair, core=1), table_high, table_low)
    return new_momentum, new_params


def band_table():
    held = {}

    def high(z, piece, term, out):
        lane = lax.broadcasted_iota(jnp.int32, (BAND, 2 * GROUP), 1)
        horiz = jnp.concatenate([term(1)[...]] * 2, axis=1)
        vert = term(0)[...]
        held["low"] = []
        for m in range(0, GROUP, 2):
            product = jnp.where(lane < GROUP, vert[:, m:m + 1], vert[:, m + 1:m + 2]) * horiz
            top, rest = split(product)
            out[:, m * GROUP:(m + 2) * GROUP] = top
            held["low"].append(rest)

    def low(z, piece, term, out):
        for i, rest in enumerate(held["low"]):
            out[:, 2 * i * GROUP:2 * (i + 1) * GROUP] = rest

    return [((BAND, GROUP * GROUP), high, BF16), ((BAND, GROUP * GROUP), low, BF16)]


def update_kernel(params_ref, packed_ref, far_ref, other_ref, far_core_ref, pair_ref, pair_core_ref, high_ref, low_ref,
                  out_ref, field, coeff, high, low, sems, out_sem):
    dp = lax.axis_index("dp")
    odd = (lax.axis_index("outer") // 2) % 2
    half = OWN // 2

    def rows(k, h, n):
        return pl.ds(((dp ^ k) * 2 + h) * (half // GROUP), n // GROUP)

    moves = [
        (pair_ref.at[0], coeff.at[:, dp]),
        (pair_ref.at[1], coeff.at[:, dp ^ 2]),
        (pair_core_ref.at[0], coeff.at[:, dp ^ 1]),
        (pair_core_ref.at[1], coeff.at[:, dp ^ 3]),
        (high_ref, high),
        (low_ref, low),
    ]
    for ref, top, n, to in (
        (params_ref, 0, OWN, rows(0, 0, OWN)),
        (packed_ref, 0, OWN, rows(1, 0, OWN)),
        (far_ref, 0, half, rows(2, odd, half)),
        (other_ref, 0, half, rows(2, 1 - odd, half)),
        (packed_ref, OWN, half, rows(3, odd, half)),
        (far_core_ref, 0, half, rows(3, 1 - odd, half)),
    ):
        for i in range(LANES):
            part = ref.at[pl.ds(top // GROUP, n // GROUP), :, pl.ds(i * 128, 128)]
            moves.append((part, field.at[i, to]))
    copies = [pltpu.make_async_copy(src, dst, sems.at[i]) for i, (src, dst) in enumerate(moves)]
    for copy in copies:
        copy.start()
    for copy in copies:
        copy.wait()
    c_high, c_low = split(coeff[...].reshape(NB * 32, BAND) * (1.0 / 8.0))
    both = jnp.concatenate([c_high, c_low], axis=0)
    lane = lax.broadcasted_iota(jnp.int32, (32, 2 * GROUP), 1)
    first = lane < GROUP
    step = 8

    def body(c, carry):
        cols = pl.ds(pl.multiple_of(c * step * GROUP, step * GROUP), step * GROUP)
        t_high = high[:, cols]
        wide = dot(both, t_high)
        value = wide[:NB * 32] + wide[NB * 32:] + dot(c_high, low[:, cols])
        for b in range(0, NB, 2):
            x0, x1 = [value[i * 32:(i + 1) * 32] for i in (b, b + 1)]
            rows_m = []
            for lt in range(step // 2):
                lanes = slice(lt * 2 * GROUP, (lt + 1) * 2 * GROUP)
                y0, y1 = x0[:, lanes], x1[:, lanes]
                rows_m.append(jnp.where(first, y0, pltpu.roll(y1, GROUP, 1)))
                rows_m.append(jnp.where(first, pltpu.roll(y0, GROUP, 1), y1))
            turned = jnp.swapaxes(jnp.stack(rows_m), 0, 1)
            at = pl.ds(pl.multiple_of(c * step, step), step)
            field[b // 2, :, at, :] = field[b // 2, :, at, :] - turned
        return carry

    lax.fori_loop(0, GROUP // step, body, 0)
    stores = [pltpu.make_async_copy(field.at[i], out_ref.at[:, :, pl.ds(i * 128, 128)], out_sem.at[i]) for i in range(LANES)]
    for store in stores:
        store.start()
    for store in stores:
        store.wait()


def update_call(*arrays):
    arrays = [a.reshape(-1, GROUP, COLS) if a.ndim == 2 and a.dtype == F32 else a for a in arrays]
    anywhere = pl.BlockSpec(memory_space=pl.ANY)
    return pl.pallas_call(
        update_kernel,
        in_specs=[anywhere] * len(arrays),
        out_specs=anywhere,
        out_shape=jax.ShapeDtypeStruct((4 * OWN // GROUP, GROUP, COLS), F32),
        scratch_shapes=[
            pltpu.VMEM((LANES, 4 * OWN // GROUP, GROUP, 128), F32),
            pltpu.VMEM((NB, 4, OWN // GROUP, BAND), F32),
            pltpu.VMEM((BAND, GROUP * GROUP), BF16),
            pltpu.VMEM((BAND, GROUP * GROUP), BF16),
            pltpu.SemaphoreType.DMA((6 + 6 * LANES,)),
            pltpu.SemaphoreType.DMA((LANES,)),
        ],
        compiler_params=pltpu.CompilerParams(vmem_limit_bytes=40 * 2**20),
        name="parameter_update",
    )(*arrays).reshape(4 * OWN, COLS)


def local(grad_parts, momentum, params, band):
    band = band.astype(jnp.int32)
    vert = cosine_columns(band // GROUP)
    horiz = cosine_columns(band % GROUP)
    new_momentum, new_params = step_rows(grad_parts, momentum[0], params, vert, horiz)
    return (new_momentum[None], new_params)


def solution(mesh):
    return jax.shard_map(
        local,
        mesh=mesh,
        in_specs=(
            P("outer", "fsdp", "dp", None, None),
            P("outer", ("fsdp", "dp"), None),
            P(("fsdp", "dp"), None),
            P(),
        ),
        out_specs=(P("outer", ("fsdp", "dp"), None), P("fsdp", None)),
        check_vma=False,
    )
```

```python
import jax
import jax.numpy as jnp
from jax import lax
from jax.experimental import pallas as pl
from jax.experimental.pallas import tpu as pltpu
from jax.sharding import PartitionSpec as P

GROUP = 64
BAND = 256
COLS = 512
NB = COLS // GROUP
OWN = 512
ZROWS = 320
FIRST = 64
LANES = COLS // 128
AXES = ("fsdp", "dp", "outer")
beta = 0.9

F32 = jnp.float32
BF16 = jnp.bfloat16


def place(x, y, z, core):
    return z * 32 + ((y // 2) * 2 + core) * 8 + x * 2 + y % 2


def swap(value, x=0, y=0, z=0, core=0):
    pairs = []
    for px in range(4):
        for py in range(4):
            for pz in range(4):
                for pc in range(2):
                    pairs.append((place(px, py, pz, pc), place(px ^ x, py ^ y, (pz + z) % 4, pc ^ core)))
    return lax.ppermute(value, AXES, pairs)


def cosine_columns(freq):
    freq = freq.astype(F32)[None, :]
    pos = jnp.arange(GROUP, dtype=F32)[:, None]
    scale = jnp.where(freq == 0, jnp.sqrt(1.0 / GROUP), jnp.sqrt(2.0 / GROUP)).astype(F32)
    return scale * jnp.cos(jnp.pi * (2.0 * pos + 1.0) * freq / (2.0 * GROUP))


def split(value):
    high = value.astype(BF16)
    return high, (value - high.astype(F32)).astype(BF16)


def dot(a, b):
    return jnp.dot(a, b, preferred_element_type=F32)


def piece_source(step, z, yh, core, parts_ref):
    f, r, c, top, rows = step
    return parts_ref.at[(z + f) % 4, (yh + r) % 2, (core + c) % 2, pl.ds(top, rows), :]


def mark(z, piece, term, out):
    out[...] = jnp.zeros((8, 128), F32)


def piece_call(name, parts, steps, terms, after, outs, cost=1):
    outs = outs + [((8, 128), mark)]
    outs = [out if len(out) == 3 else out + (F32,) for out in outs]
    n_terms, n_after, n_outs, n_steps = len(terms), len(after), len(outs), len(steps)
    picked = [i for i, t in enumerate(terms) if isinstance(t, tuple)]

    def kernel(parts_ref, *refs):
        refs = list(refs)
        take = lambda n: [refs.pop(0) for _ in range(n)]
        term_refs, _, out_refs = take(n_terms), take(n_after), take(n_outs)
        bufs, held, sems = take(n_steps), take(len(picked)), take(n_steps + len(picked))
        z, dp, x = lax.axis_index("fsdp"), lax.axis_index("dp"), lax.axis_index("outer") // 2
        sources = [piece_source(s, z, dp // 2, dp % 2, parts_ref) for s in steps]
        sources += [terms[i][2](x, term_refs[i]) for i in picked]
        loads = []
        for src, buf, sem in zip(sources, bufs + held, sems):
            copy = pltpu.make_async_copy(src, buf, sem)
            copy.start()
            loads.append(copy)
        waiting = set(range(len(loads)))

        def loaded(i):
            if i in waiting:
                waiting.remove(i)
                loads[i].wait()
            return (bufs + held)[i]

        def term(i):
            return loaded(n_steps + picked.index(i)) if i in picked else term_refs[i]

        for (_, body, _), ref in zip(outs, out_refs):
            body(z, loaded, term, ref)
        for i in sorted(waiting):
            loads[i].wait()

    here, anywhere = pl.BlockSpec(memory_space=pltpu.VMEM), pl.BlockSpec(memory_space=pl.ANY)
    hold = lambda v: pltpu.with_memory_space_constraint(v, pltpu.VMEM)
    return pl.pallas_call(
        kernel,
        in_specs=[pl.BlockSpec(memory_space=pltpu.HBM)] + [anywhere if i in picked else here for i in range(n_terms)]
        + [anywhere] * n_after,
        out_specs=[here] * n_outs,
        out_shape=[pltpu.VMEM(s, t) for s, _, t in outs],
        scratch_shapes=[pltpu.VMEM((s[4], COLS), BF16) for s in steps]
        + [pltpu.VMEM(terms[i][1], F32) for i in picked]
        + [pltpu.SemaphoreType.DMA] * (n_steps + len(picked)),
        compiler_params=pltpu.CompilerParams(vmem_limit_bytes=24 * 2**20),
        cost_estimate=pl.CostEstimate(flops=1, bytes_accessed=cost, transcendentals=0),
        name=name,
    )(parts, *[t[0] if i in picked else hold(t) for i, t in enumerate(terms)], *after)


def encode(mom, vert, horiz):
    rows = mom.shape[0]
    w_high, w_low = split(horiz)
    x_high, x_low = split(mom)
    out = []
    for b in range(NB):
        cut = slice(b * GROUP, (b + 1) * GROUP)
        half = dot(x_high[:, cut], w_high) + dot(x_low[:, cut], w_high) + dot(x_high[:, cut], w_low)
        out.append(jnp.sum(half.reshape(rows // GROUP, GROUP, BAND) * vert[None], axis=1))
    return out


def step_rows(grad_parts, momentum, params, vert, horiz):
    parts = pltpu.with_memory_space_constraint(grad_parts.reshape(4, 2, 2, OWN, COLS), pltpu.HBM)
    vert_t, horiz_t = vert.T, horiz.T
    zr, yr, half = ZROWS, OWN - ZROWS, COLS // 2
    left, right = slice(0, half), slice(half, COLS)
    call = lambda name, *rest, **options: piece_call(name, parts, *rest, **options)
    up, down = (lambda v: swap(v, z=1)), (lambda v: swap(v, z=3))
    OPP, UP, DOWN, MINE = 2, 1, 3, 0

    def z_rows(f, r, c):
        return (f, r, c, 0, zr)

    def y_rows(f, r, c):
        return (f, r, c, zr, yr)

    def widen(name, groups, after):
        outs, first = [], 0
        for group in groups:
            def body(z, piece, term, out, group=group, first=first):
                top = 0
                for i, step in enumerate(group):
                    out[top:top + step[4], :] = piece(first + i)[...].astype(F32)
                    top += step[4]

            outs.append(((sum(s[4] for s in group), COLS), body))
            first += len(group)
        return call(name, [s for group in groups for s in group], [], after, outs)

    def add(i_pieces, i_term, first, cols=slice(None), half_terms=(), full_terms=()):
        def run(z, piece, term, out):
            top = 0
            for i in i_pieces:
                n = piece(i).shape[0]
                cut = slice(top, top + n)
                value = term(i_term)[first + top:first + top + n, cols] + piece(i)[:, cols].astype(F32)
                for k in full_terms:
                    value = value + term(k)[cut, cols]
                for k in half_terms:
                    value = value + term(k)[cut]
                out[cut, :] = value
                top += n
        return run

    def side(i_pieces, i_term, first, h_add, i_add):
        def run(z, piece, term, out):
            for h, cols in enumerate((left, right)):
                body = add(i_pieces, i_term, first, cols, (i_add,) if h == h_add else ())
                body(z, piece, term, out.at[:, cols])
        return run

    def pack(z, piece, term, out):
        odd = (lax.axis_index("outer") // 2) % 2
        n = OWN // 2
        out[:OWN, :] = term(0)[...]
        out[pl.ds(pl.multiple_of(OWN + odd * n, n), n), :] = term(1)[...]
        out[pl.ds(pl.multiple_of(OWN + (1 - odd) * n, n), n), :] = term(2)[...]

    w_first, ta = widen("widen_a", [[z_rows(OPP, 0, 1), z_rows(OPP, 1, 1), y_rows(OPP, 1, 1)]], [])
    c_first = swap(w_first, core=1)
    *w_b, tb = widen("widen_b", [
        [z_rows(UP, 0, 1), z_rows(UP, 1, 1)], [z_rows(DOWN, 0, 1), z_rows(DOWN, 1, 1)],
        [y_rows(UP, 1, 1), y_rows(DOWN, 1, 1), y_rows(MINE, 1, 1), y_rows(OPP, 0, 1)],
        [z_rows(MINE, 0, 1), z_rows(MINE, 1, 1)],
        [y_rows(UP, 0, 1), y_rows(DOWN, 0, 1), y_rows(MINE, 0, 1)]], [ta])
    c_up, c_down, c_cross, c_own, c_rest = [swap(w, core=1) for w in w_b]
    def params_part(top, n):
        def pick(x, ref):
            return ref.at[pl.ds(pl.multiple_of((x % 2) * (OWN // 2) + top, 64), n), :]
        return (params, (n, COLS), pick)

    def with_params(body, i_params):
        def run(z, piece, term, out):
            n = out.shape[0] - term(i_params).shape[0]
            body(z, piece, term, out.at[:n])
            out[n:, :] = term(i_params)[...]
        return run

    u1, d1, y1, t1 = call(
        "opposite", [z_rows(OPP, 0, 0), z_rows(OPP, 1, 0), y_rows(OPP, 1, 0)], [c_first, params_part(0, FIRST)], [tb],
        [((2 * zr, half), add((0, 1), 0, 0, left)), ((2 * zr, half), add((0, 1), 0, 0, right)),
         ((yr + FIRST, COLS), with_params(add((2,), 0, 2 * zr), 1))])
    gu1, gd1, gy1 = up(u1), down(d1), swap(y1, y=2)

    table_high, table_low, tt = call("band_table", [], [vert_t, horiz_t], [t1], band_table())
    fold = yr // 2

    def onward(i, first, h_add, i_add, cols):
        def run(z, piece, term, out):
            side((2 * i, 2 * i + 1), i, 0, h_add, i_add)(z, piece, term, out.at[:2 * zr])
            value = term(4)[3 * yr:, cols] + term(5)[:yr, cols] + piece(7)[:, cols].astype(F32)
            out[2 * zr:, left] = value[:fold]
            out[2 * zr:, right] = value[fold:]
        return run

    u2, d2, y2, t2 = call(
        "sides", [z_rows(UP, 0, 0), z_rows(UP, 1, 0), z_rows(DOWN, 0, 0), z_rows(DOWN, 1, 0),
                  y_rows(UP, 1, 0), y_rows(DOWN, 1, 0), y_rows(MINE, 1, 0), y_rows(OPP, 0, 0)],
        [c_up, c_down, gu1, gd1, c_cross, gy1, params_part(FIRST, OWN // 2 - FIRST)], [tt],
        [((2 * zr + fold, COLS), onward(0, 0, 0, 2, left)), ((2 * zr + fold, COLS), onward(1, 0, 1, 3, right)),
         ((3 * yr + OWN // 2 - FIRST, COLS), with_params(add((4, 5, 6), 4, 0), 6))])
    gu2, gd2, gy2 = up(u2), down(d2), swap(y2, y=2)

    def own_body(r):
        def run(z, piece, term, out):
            cut = slice(r * zr, (r + 1) * zr)
            out[...] = term(0)[cut] + piece(r)[...].astype(F32) + (term(1)[cut] + term(2)[cut])
        return run

    def last_side(i, h_add, i_add):
        def run(z, piece, term, out):
            cut = slice(i * yr, (i + 1) * yr)
            for h, cols in enumerate((left, right)):
                value = term(3)[cut, cols] + term(4)[cut, cols] + piece(2 + i)[:, cols].astype(F32)
                if h == h_add:
                    out[:fold, cols] = value[:fold] + term(i_add)[2 * zr:, left]
                    out[fold:, cols] = value[fold:] + term(i_add)[2 * zr:, right]
                else:
                    out[:, cols] = value
        return run

    def last_own_body(z, piece, term, out):
        out[...] = term(3)[2 * yr:3 * yr] + term(4)[2 * yr:] + piece(4)[...].astype(F32)

    def far_body(z, piece, term, out):
        out[:FIRST, :] = term(5)[yr:, :]
        out[FIRST:, :] = term(3)[3 * yr:, :]

    y3, u4, d4, near, last_own, far_half, t6 = call(
        "own", [z_rows(MINE, 0, 0), z_rows(MINE, 1, 0), y_rows(UP, 0, 0), y_rows(DOWN, 0, 0), y_rows(MINE, 0, 0)],
        [c_own, gu2, gd2, gy2, c_rest, gy1], [t2],
        [((zr, COLS), own_body(1)), ((yr, COLS), last_side(0, 0, 1)), ((yr, COLS), last_side(1, 1, 2)),
         ((zr, COLS), own_body(0)), ((yr, COLS), last_own_body),
         ((OWN // 2, COLS), far_body)])
    far_other = swap(far_half, x=1)
    gy3, gu4, gd4 = swap(y3, y=2), up(u4), down(d4)
    def momentum_rows(top, n):
        return (momentum, (n, COLS), lambda x, ref: ref.at[pl.ds(top, n), :])

    def near_mom(z, piece, term, out):
        out[...] = beta * term(2)[...] + (term(0)[...] + term(1)[...]) * (1.0 / 16.0)
        near_mom.value = out

    def near_shared(z, piece, term, out):
        for b, value in enumerate(encode(near_mom.value[...], term(3)[...], term(4)[...])):
            out[b] = value

    nz, ny = zr // GROUP, yr // GROUP
    mom_top, shared_top, t7 = call(
        "near_momentum", [], [near, gy3, momentum_rows(0, zr), vert, horiz], [t6],
        [((zr, COLS), near_mom), ((NB, nz, BAND), near_shared)], cost=9 * 10**6,
    )

    def last_mom(z, piece, term, out):
        grad = term(0)[...] + (term(1)[...] + term(2)[...])
        out[...] = beta * term(3)[...] + grad * (1.0 / 16.0)
        last_mom.value = out

    def last_shared(z, piece, term, out):
        for b, value in enumerate(encode(last_mom.value[...], term(4)[...], term(5)[...])):
            out[b, :nz, :] = term(6)[b]
            out[b, nz:, :] = value

    mom_low, shared, t8 = call(
        "last_momentum", [], [last_own, gu4, gd4, momentum_rows(zr, yr), vert, horiz, shared_top], [t7],
        [((yr, COLS), last_mom), ((NB, nz + ny, BAND), last_shared)],
    )

    packed, _ = call("params_pack", [], [params, far_half, far_other], [t8], [((2 * OWN, COLS), pack)])
    packed_core = swap(packed, core=1)

    def residual(z, piece, term, out):
        high, low = split(term(4)[...])
        w_both = jnp.concatenate([high, low], axis=1)
        vert_now = term(3)[...][None]
        for pair in range(NB // 2):
            sides = []
            for b in (2 * pair, 2 * pair + 1):
                wide = (term(2)[b][:, None, :] * vert_now).reshape(OWN, BAND)
                wide_high, wide_low = split(wide)
                both = dot(wide_high, w_both)
                sides.append(both[:, :GROUP] + both[:, GROUP:] + dot(wide_low, w_both[:, :GROUP]))
            cols = slice(pair * 2 * GROUP, (pair + 1) * 2 * GROUP)
            value = jnp.concatenate(sides, axis=1)
            out[:zr, cols] = term(0)[:, cols] - value[:zr]
            out[zr:, cols] = term(1)[:, cols] - value[zr:]

    new_momentum, t9 = call("momentum_residual", [], [mom_top, mom_low, shared, vert, horiz_t], [t8],
                            [((OWN, COLS), residual)], cost=9 * 10**6)

    def sum_four(z, piece, term, out):
        out[...] = (term(0)[...] + term(1)[...]) + (term(2)[...] + term(3)[...])

    def sum_pairs(z, piece, term, out):
        out[0] = term(0)[...] + term(1)[...]
        out[1] = term(2)[...] + term(3)[...]

    total, t10 = call("sum_x", [], [shared] + [swap(shared, x=k) for k in (1, 2, 3)], [t9], [(shared.shape, sum_four)])
    pair, _ = call("sum_y", [], [total] + [swap(total, y=k) for k in (1, 2, 3)], [], [((2,) + shared.shape, sum_pairs)])
    new_params = update_call(packed, packed_core, pair, swap(pair, core=1), table_high, table_low)
    return new_momentum, new_params


def band_table():
    held = {}

    def high(z, piece, term, out):
        lane = lax.broadcasted_iota(jnp.int32, (BAND, 2 * GROUP), 1)
        horiz = jnp.concatenate([term(1)[...]] * 2, axis=1)
        vert = term(0)[...]
        held["low"] = []
        for m in range(0, GROUP, 2):
            product = jnp.where(lane < GROUP, vert[:, m:m + 1], vert[:, m + 1:m + 2]) * horiz
            top, rest = split(product)
            out[:, m * GROUP:(m + 2) * GROUP] = top
            held["low"].append(rest)

    def low(z, piece, term, out):
        for i, rest in enumerate(held["low"]):
            out[:, 2 * i * GROUP:2 * (i + 1) * GROUP] = rest

    return [((BAND, GROUP * GROUP), high, BF16), ((BAND, GROUP * GROUP), low, BF16)]


def update_kernel(rows_ref, rows_core_ref, pair_ref, pair_core_ref, high_ref, low_ref, out_ref, coeff, field, sems):
    dp = lax.axis_index("dp")
    nblock = OWN // GROUP
    for k in range(4):
        coeff[:, k] = (pair_ref, pair_core_ref)[k % 2][k // 2]
    c_high, c_low = split(coeff[...].reshape(NB * 4 * nblock, BAND) * (1.0 / 8.0))
    both = jnp.concatenate([c_high, c_low], axis=0)
    lane = lax.broadcasted_iota(jnp.int32, (4 * nblock, 2 * GROUP), 1)
    first = lane < GROUP
    step = 8
    stores = []
    for c in range(GROUP // step):
        cols = slice(c * step * GROUP, (c + 1) * step * GROUP)
        wide = dot(both, high_ref[:, cols])
        value = wide[:NB * 4 * nblock] + wide[NB * 4 * nblock:] + dot(c_high, low_ref[:, cols])
        at = slice(c * step, (c + 1) * step)
        for b in range(0, NB, 2):
            x0, x1 = [value[i * 4 * nblock:(i + 1) * 4 * nblock] for i in (b, b + 1)]
            rows_m = []
            for lt in range(step // 2):
                lanes = slice(lt * 2 * GROUP, (lt + 1) * 2 * GROUP)
                y0, y1 = x0[:, lanes], x1[:, lanes]
                rows_m.append(jnp.where(first, y0, pltpu.roll(y1, GROUP, 1)))
                rows_m.append(jnp.where(first, pltpu.roll(y0, GROUP, 1), y1))
            turned = jnp.swapaxes(jnp.stack(rows_m), 0, 1)
            out_cols = slice(b * GROUP, (b + 2) * GROUP)
            for k in range(4):
                held = (rows_ref, rows_core_ref)[k % 2][k // 2, :, at, out_cols]
                field[k, :, at, out_cols] = held - turned[k * nblock:(k + 1) * nblock]
        for k in range(4):
            store = pltpu.make_async_copy(field.at[k, :, pl.ds(c * step, step), :],
                                          out_ref.at[dp ^ k, :, pl.ds(c * step, step), :], sems.at[c * 4 + k])
            store.start()
            stores.append(store)
    for store in stores:
        store.wait()


def update_call(rows, rows_core, *arrays):
    shape = (2, OWN // GROUP, GROUP, COLS)
    arrays = (rows.reshape(shape), rows_core.reshape(shape)) + arrays
    return pl.pallas_call(
        update_kernel,
        in_specs=[pl.BlockSpec(memory_space=pltpu.VMEM)] * len(arrays),
        out_specs=pl.BlockSpec(memory_space=pl.ANY),
        out_shape=jax.ShapeDtypeStruct((4, OWN // GROUP, GROUP, COLS), F32),
        scratch_shapes=[
            pltpu.VMEM((NB, 4, OWN // GROUP, BAND), F32),
            pltpu.VMEM((4, OWN // GROUP, GROUP, COLS), F32),
            pltpu.SemaphoreType.DMA((4 * GROUP // 8,)),
        ],
        compiler_params=pltpu.CompilerParams(vmem_limit_bytes=24 * 2**20),
        name="parameter_update",
    )(*[pltpu.with_memory_space_constraint(a, pltpu.VMEM) for a in arrays]).reshape(4 * OWN, COLS)


def local(grad_parts, momentum, params, band):
    band = band.astype(jnp.int32)
    vert = cosine_columns(band // GROUP)
    horiz = cosine_columns(band % GROUP)
    new_momentum, new_params = step_rows(grad_parts, momentum[0], params, vert, horiz)
    return (new_momentum[None], new_params)


def solution(mesh):
    return jax.shard_map(
        local,
        mesh=mesh,
        in_specs=(
            P("outer", "fsdp", "dp", None, None),
            P("outer", ("fsdp", "dp"), None),
            P(("fsdp", "dp"), None),
            P(),
        ),
        out_specs=(P("outer", ("fsdp", "dp"), None), P("fsdp", None)),
        check_vma=False,
    )
```

```python
import jax
import jax.numpy as jnp
from jax import lax
from jax.experimental import pallas as pl
from jax.experimental.pallas import tpu as pltpu
from jax.sharding import PartitionSpec as P

GROUP = 64
BAND = 256
COLS = 512
NB = COLS // GROUP
OWN = 512
ZROWS = 320
FIRST = 32
LANES = COLS // 128
AXES = ("fsdp", "dp", "outer")
beta = 0.9

F32 = jnp.float32
BF16 = jnp.bfloat16


def place(x, y, z, core):
    return z * 32 + ((y // 2) * 2 + core) * 8 + x * 2 + y % 2


def swap(value, x=0, y=0, z=0, core=0):
    pairs = []
    for px in range(4):
        for py in range(4):
            for pz in range(4):
                for pc in range(2):
                    pairs.append((place(px, py, pz, pc), place(px ^ x, py ^ y, (pz + z) % 4, pc ^ core)))
    return lax.ppermute(value, AXES, pairs)


def cosine_columns(freq):
    freq = freq.astype(F32)[None, :]
    pos = jnp.arange(GROUP, dtype=F32)[:, None]
    scale = jnp.where(freq == 0, jnp.sqrt(1.0 / GROUP), jnp.sqrt(2.0 / GROUP)).astype(F32)
    return scale * jnp.cos(jnp.pi * (2.0 * pos + 1.0) * freq / (2.0 * GROUP))


def split(value):
    high = value.astype(BF16)
    return high, (value - high.astype(F32)).astype(BF16)


def dot(a, b):
    return jnp.dot(a, b, preferred_element_type=F32)


def piece_source(step, z, yh, core, parts_ref):
    f, r, c, top, rows = step
    return parts_ref.at[(z + f) % 4, (yh + r) % 2, (core + c) % 2, pl.ds(top, rows), :]


def mark(z, piece, term, out):
    out[...] = jnp.zeros((8, 128), F32)


def piece_call(name, parts, steps, terms, after, outs, cost=1, result=False):
    outs = outs + [((8, 128), mark)]
    outs = [out if len(out) == 3 else out + (F32,) for out in outs]
    n_terms, n_after, n_outs, n_steps = len(terms), len(after), len(outs), len(steps)
    picked = [i for i, t in enumerate(terms) if isinstance(t, tuple)]

    def kernel(parts_ref, *refs):
        refs = list(refs)
        take = lambda n: [refs.pop(0) for _ in range(n)]
        term_refs, _, out_refs = take(n_terms), take(n_after), take(n_outs)
        bufs, held, sems = take(n_steps), take(len(picked)), take(n_steps + len(picked))
        z, dp, x = lax.axis_index("fsdp"), lax.axis_index("dp"), lax.axis_index("outer") // 2
        sources = [piece_source(s, z, dp // 2, dp % 2, parts_ref) for s in steps]
        sources += [terms[i][2](x, term_refs[i]) for i in picked]
        loads = []
        for src, buf, sem in zip(sources, bufs + held, sems):
            copy = pltpu.make_async_copy(src, buf, sem)
            copy.start()
            loads.append(copy)
        waiting = set(range(len(loads)))

        def loaded(i):
            if i in waiting:
                waiting.remove(i)
                loads[i].wait()
            return (bufs + held)[i]

        def term(i):
            return loaded(n_steps + picked.index(i)) if i in picked else term_refs[i]

        for (_, body, _), ref in zip(outs, out_refs):
            body(z, loaded, term, ref)
        for i in sorted(waiting):
            loads[i].wait()

    here, anywhere = pl.BlockSpec(memory_space=pltpu.VMEM), pl.BlockSpec(memory_space=pl.ANY)
    hold = lambda v: pltpu.with_memory_space_constraint(v, pltpu.VMEM)
    return pl.pallas_call(
        kernel,
        in_specs=[pl.BlockSpec(memory_space=pltpu.HBM)] + [anywhere if i in picked else here for i in range(n_terms)]
        + [anywhere] * n_after,
        out_specs=[here] * n_outs,
        out_shape=[(jax.ShapeDtypeStruct if result and i == 0 else pltpu.VMEM)(s, t) for i, (s, _, t) in enumerate(outs)],
        scratch_shapes=[pltpu.VMEM((s[4], COLS), BF16) for s in steps]
        + [pltpu.VMEM(terms[i][1], F32) for i in picked]
        + [pltpu.SemaphoreType.DMA] * (n_steps + len(picked)),
        compiler_params=pltpu.CompilerParams(vmem_limit_bytes=24 * 2**20),
        cost_estimate=pl.CostEstimate(flops=cost*100, bytes_accessed=cost, transcendentals=0),
        name=name,
    )(parts, *[t[0] if i in picked else hold(t) for i, t in enumerate(terms)], *after)


def encode(mom, vert, horiz):
    rows = mom.shape[0]
    w_high, w_low = split(horiz)
    x_high, x_low = split(mom)
    out = []
    for b in range(NB):
        cut = slice(b * GROUP, (b + 1) * GROUP)
        half = dot(x_high[:, cut], w_high) + dot(x_low[:, cut], w_high) + dot(x_high[:, cut], w_low)
        out.append(jnp.sum(half.reshape(rows // GROUP, GROUP, BAND) * vert[None], axis=1))
    return out


def step_rows(grad_parts, momentum, params, vert, horiz):
    parts = pltpu.with_memory_space_constraint(grad_parts.reshape(4, 2, 2, OWN, COLS), pltpu.HBM)
    vert_t, horiz_t = vert.T, horiz.T
    zr, yr, half = ZROWS, OWN - ZROWS, COLS // 2
    left, right = slice(0, half), slice(half, COLS)
    call = lambda name, *rest, **options: piece_call(name, parts, *rest, **options)
    up, down = (lambda v: swap(v, z=1)), (lambda v: swap(v, z=3))
    OPP, UP, DOWN, MINE = 2, 1, 3, 0

    def z_rows(f, r, c):
        return (f, r, c, 0, zr)

    def y_rows(f, r, c):
        return (f, r, c, zr, yr)

    def widen(name, groups, after, more=None):
        extra = 0 if more is None else more.shape[0]
        outs, first = [], 0
        for group in groups:
            tail = extra if group is groups[-1] else 0

            def body(z, piece, term, out, group=group, first=first, tail=tail):
                top = 0
                for i, step in enumerate(group):
                    out[top:top + step[4], :] = piece(first + i)[...].astype(F32)
                    top += step[4]
                if tail:
                    out[top:, :] = term(0)[...]

            outs.append(((sum(s[4] for s in group) + tail, COLS), body))
            first += len(group)
        return call(name, [s for group in groups for s in group], [] if more is None else [more], after, outs)

    def add(i_pieces, i_term, first, cols=slice(None), half_terms=(), full_terms=()):
        def run(z, piece, term, out):
            top = 0
            for i in i_pieces:
                n = piece(i).shape[0]
                cut = slice(top, top + n)
                value = term(i_term)[first + top:first + top + n, cols] + piece(i)[:, cols].astype(F32)
                for k in full_terms:
                    value = value + term(k)[cut, cols]
                for k in half_terms:
                    value = value + term(k)[cut]
                out[cut, :] = value
                top += n
        return run

    def side(i_pieces, i_term, first, h_add, i_add):
        def run(z, piece, term, out):
            for h, cols in enumerate((left, right)):
                body = add(i_pieces, i_term, first, cols, (i_add,) if h == h_add else ())
                body(z, piece, term, out.at[:, cols])
        return run

    w_first, ta = widen("widen_a", [[z_rows(OPP, 0, 1), z_rows(OPP, 1, 1), y_rows(OPP, 1, 1)]], [])
    c_first = swap(w_first, core=1)
    *w_b, tb = widen("widen_b", [
        [z_rows(UP, 0, 1), z_rows(UP, 1, 1)], [z_rows(DOWN, 0, 1), z_rows(DOWN, 1, 1)],
        [y_rows(UP, 1, 1), y_rows(DOWN, 1, 1), y_rows(MINE, 1, 1), y_rows(OPP, 0, 1)],
        [z_rows(MINE, 0, 1), z_rows(MINE, 1, 1)],
        [y_rows(UP, 0, 1), y_rows(DOWN, 0, 1), y_rows(MINE, 0, 1)]], [ta], params)
    c_up, c_down, c_cross, c_own, c_rest = [swap(w, core=1) for w in w_b]
    def params_part(top, n):
        def pick(x, ref):
            return ref.at[pl.ds(pl.multiple_of((x % 2) * (OWN // 2) + top, FIRST), n), :]
        return (params, (n, COLS), pick)

    def with_params(body, i_params):
        def run(z, piece, term, out):
            n = out.shape[0] - term(i_params).shape[0]
            body(z, piece, term, out.at[:n])
            out[n:, :] = term(i_params)[...]
        return run

    u1, d1, y1, t1 = call(
        "opposite", [z_rows(OPP, 0, 0), z_rows(OPP, 1, 0), y_rows(OPP, 1, 0)], [c_first, params_part(0, FIRST)], [tb],
        [((2 * zr, half), add((0, 1), 0, 0, left)), ((2 * zr, half), add((0, 1), 0, 0, right)),
         ((yr + FIRST, COLS), with_params(add((2,), 0, 2 * zr), 1))])
    gu1, gd1, gy1 = up(u1), down(d1), swap(y1, y=2)

    table_high, table_low, tt = call("band_table", [], [vert_t, horiz_t], [t1], band_table())
    fold = yr // 2

    def onward(i, first, h_add, i_add, cols):
        def run(z, piece, term, out):
            side((2 * i, 2 * i + 1), i, 0, h_add, i_add)(z, piece, term, out.at[:2 * zr])
            value = term(4)[3 * yr:, cols] + term(5)[:yr, cols] + piece(7)[:, cols].astype(F32)
            out[2 * zr:, left] = value[:fold]
            out[2 * zr:, right] = value[fold:]
        return run

    u2, d2, y2, t2 = call(
        "sides", [z_rows(UP, 0, 0), z_rows(UP, 1, 0), z_rows(DOWN, 0, 0), z_rows(DOWN, 1, 0),
                  y_rows(UP, 1, 0), y_rows(DOWN, 1, 0), y_rows(MINE, 1, 0), y_rows(OPP, 0, 0)],
        [c_up, c_down, gu1, gd1, c_cross, gy1, params_part(FIRST, OWN // 2 - FIRST)], [tt],
        [((2 * zr + fold, COLS), onward(0, 0, 0, 2, left)), ((2 * zr + fold, COLS), onward(1, 0, 1, 3, right)),
         ((3 * yr + OWN // 2 - FIRST, COLS), with_params(add((4, 5, 6), 4, 0), 6))])
    gu2, gd2, gy2 = up(u2), down(d2), swap(y2, y=2)

    def own_body(r):
        def run(z, piece, term, out):
            cut = slice(r * zr, (r + 1) * zr)
            out[...] = term(0)[cut] + piece(r)[...].astype(F32) + (term(1)[cut] + term(2)[cut])
        return run

    def last_side(i, h_add, i_add):
        def run(z, piece, term, out):
            cut = slice(i * yr, (i + 1) * yr)
            for h, cols in enumerate((left, right)):
                value = term(3)[cut, cols] + term(4)[cut, cols] + piece(2 + i)[:, cols].astype(F32)
                if h == h_add:
                    out[:fold, cols] = value[:fold] + term(i_add)[2 * zr:, left]
                    out[fold:, cols] = value[fold:] + term(i_add)[2 * zr:, right]
                else:
                    out[:, cols] = value
        return run

    def last_own_body(z, piece, term, out):
        out[...] = term(3)[2 * yr:3 * yr] + term(4)[2 * yr:3 * yr] + piece(4)[...].astype(F32)

    def far_body(z, piece, term, out):
        out[:FIRST, :] = term(5)[yr:, :]
        out[FIRST:, :] = term(3)[3 * yr:, :]

    far_rows, u4, d4, near, last_own, far_half, t6 = call(
        "own", [z_rows(MINE, 0, 0), z_rows(MINE, 1, 0), y_rows(UP, 0, 0), y_rows(DOWN, 0, 0), y_rows(MINE, 0, 0)],
        [c_own, gu2, gd2, gy2, c_rest, gy1], [t2],
        [((zr, COLS), own_body(1)), ((yr, COLS), last_side(0, 0, 1)), ((yr, COLS), last_side(1, 1, 2)),
         ((zr, COLS), own_body(0)), ((yr, COLS), last_own_body),
         ((OWN // 2, COLS), far_body)])
    far_other = swap(far_half, x=1)
    from_core = [swap(far_half, core=1)]
    gu4, gd4 = up(u4), down(d4)
    def momentum_rows(top, n):
        return (momentum, (n, COLS), lambda x, ref: ref.at[pl.ds(top, n), :])

    nz, ny = zr // GROUP, yr // GROUP

    def near_partial(z, piece, term, out):
        value = beta * term(2)[...] + term(0)[...] * (1.0 / 16.0)
        for b, (mine, theirs) in enumerate(zip(encode(value, term(3)[...], term(4)[...]),
                                               encode(term(1)[...] * (1.0 / 16.0), term(3)[...], term(4)[...]))):
            out[b, :nz, :] = mine
            out[b, nz:, :] = theirs

    def hand_on(z, piece, term, out):
        out[...] = term(1)[...]

    partial, y3, _ = call("partial_encode", [], [near, far_rows, momentum_rows(0, zr), vert, horiz], [t6],
                        [((NB, 2 * nz, BAND), near_partial), ((zr, COLS), hand_on)])
    gy3 = swap(y3, y=2)

    def last_mom(z, piece, term, out):
        grad = term(0)[...] + (term(1)[...] + term(2)[...])
        out[...] = beta * term(3)[...] + grad * (1.0 / 16.0)
        last_mom.value = out

    def last_coeffs(z, piece, term, out):
        for b, value in enumerate(encode(last_mom.value[...], term(4)[...], term(5)[...])):
            out[b, :nz, :] = term(6)[b, :nz]
            out[b, nz:nz + ny, :] = value
            out[b, nz + ny:, :] = term(6)[b, nz:]

    mom_low, coeffs, t7 = call(
        "last_momentum", [], [last_own, gu4, gd4, momentum_rows(zr, yr), vert, horiz, partial], [t6, far_other, from_core[0]],
        [((yr, COLS), last_mom), ((NB, 2 * nz + ny, BAND), last_coeffs)], cost=4 * 10**6,
    )

    def sum_four(z, piece, term, out):
        out[...] = (term(0)[...] + term(2)[...]) + (term(1)[...] + term(3)[...])

    total, tx = call("sum_x", [], [coeffs] + [swap(coeffs, x=k) for k in (2, 1, 3)], [], [(coeffs.shape, sum_four)],
                    cost=20000000)
    def near_mom(z, piece, term, out):
        out[...] = beta * term(2)[...] + (term(0)[...] + term(1)[...]) * (1.0 / 16.0)
        near_mom.value = out

    def near_shared(z, piece, term, out):
        for b, value in enumerate(encode(near_mom.value[...], term(3)[...], term(4)[...])):
            out[b, :nz, :] = value
            out[b, nz:, :] = term(5)[b, nz:nz + ny]

    def far_copy(z, piece, term, out):
        out[...] = term(6)[...]

    mom_top, shared, far_late, t8 = call(
        "near_momentum", [], [near, gy3, momentum_rows(0, zr), vert, horiz, coeffs, far_other], [tx],
        [((zr, COLS), near_mom), ((NB, nz + ny, BAND), near_shared), ((OWN // 2, COLS), far_copy)], cost=5 * 10**6,
    )
    from_core.append(swap(far_late, core=1))

    def residual(z, piece, term, out):
        high, low = split(term(4)[...])
        w_both = jnp.concatenate([high, low], axis=1)
        vert_now = term(3)[...][None]
        for pair in range(NB // 2):
            sides = []
            for b in (2 * pair, 2 * pair + 1):
                wide = (term(2)[b][:, None, :] * vert_now).reshape(OWN, BAND)
                wide_high, wide_low = split(wide)
                both = dot(wide_high, w_both)
                sides.append(both[:, :GROUP] + both[:, GROUP:] + dot(wide_low, w_both[:, :GROUP]))
            cols = slice(pair * 2 * GROUP, (pair + 1) * 2 * GROUP)
            value = jnp.concatenate(sides, axis=1)
            out[:zr, cols] = term(0)[:, cols] - value[:zr]
            out[zr:, cols] = term(1)[:, cols] - value[zr:]

    new_momentum, t9 = call("momentum_residual", [], [mom_top, mom_low, shared, vert, horiz_t], [t8],
                            [((OWN, COLS), residual)], cost=9 * 10**6, result=True)

    def sum_pairs(z, piece, term, out):
        top, low, far = slice(0, nz), slice(nz, nz + ny), slice(nz + ny, None)
        for k, (a, b, c, d) in enumerate(((0, 2, 1, 3), (1, 3, 0, 2))):
            own = [term(a)[:, cut] + term(b)[:, cut] for cut in (top, low)]
            out[k, :, :nz, :] = own[0] + (term(c)[:, far] + term(d)[:, far])
            out[k, :, nz:, :] = own[1]

    pair, _ = call("sum_y", [], [total] + [swap(total, y=k) for k in (2, 1, 3)], [t9], [((2,) + shared.shape, sum_pairs)],
                   cost=7 * 10**7)
    new_params = update_call([params, far_half, far_other, c_rest] + from_core, pair, swap(pair, core=1), table_high, table_low)
    return new_momentum, new_params


def band_table():
    held = {}

    def high(z, piece, term, out):
        lane = lax.broadcasted_iota(jnp.int32, (BAND, 2 * GROUP), 1)
        horiz = jnp.concatenate([term(1)[...]] * 2, axis=1)
        vert = term(0)[...]
        held["low"] = []
        for m in range(0, GROUP, 2):
            product = jnp.where(lane < GROUP, vert[:, m:m + 1], vert[:, m + 1:m + 2]) * horiz
            top, rest = split(product)
            out[:, m * GROUP:(m + 2) * GROUP] = top
            held["low"].append(rest)

    def low(z, piece, term, out):
        for i, rest in enumerate(held["low"]):
            out[:, 2 * i * GROUP:2 * (i + 1) * GROUP] = rest

    return [((BAND, GROUP * GROUP), high, BF16), ((BAND, GROUP * GROUP), low, BF16)]


def update_kernel(own_ref, far_ref, other_ref, core_own_ref, core_far_ref, core_other_ref,
                  pair_ref, pair_core_ref, high_ref, low_ref, out_ref, coeff, field, sems):
    dp = lax.axis_index("dp")
    odd = (lax.axis_index("outer") // 2) % 2
    nblock = OWN // GROUP
    part = nblock // 2
    core_own = core_own_ref.at[core_own_ref.shape[0] - nblock:]
    rows = ((own_ref,), (core_own,), (far_ref, other_ref), (core_far_ref, core_other_ref))
    for k in range(4):
        value = (pair_ref, pair_core_ref)[k % 2][k // 2]
        if k >= 2:
            turned = jnp.concatenate([value[:, part:], value[:, :part]], axis=1)
            value = jnp.where(odd == 1, turned, value)
        coeff[:, k] = value
    c_high, c_low = split(coeff[...].reshape(NB * 4 * nblock, BAND) * (1.0 / 8.0))
    both = jnp.concatenate([c_high, c_low], axis=0)
    lane = lax.broadcasted_iota(jnp.int32, (4 * nblock, 2 * GROUP), 1)
    first = lane < GROUP
    step = 8
    stores = []
    for c in range(GROUP // step):
        cols = slice(c * step * GROUP, (c + 1) * step * GROUP)
        wide = dot(both, high_ref[:, cols])
        value = wide[:NB * 4 * nblock] + wide[NB * 4 * nblock:] + dot(c_high, low_ref[:, cols])
        at = slice(c * step, (c + 1) * step)
        for b in range(0, NB, 2):
            x0, x1 = [value[i * 4 * nblock:(i + 1) * 4 * nblock] for i in (b, b + 1)]
            rows_m = []
            for lt in range(step // 2):
                lanes = slice(lt * 2 * GROUP, (lt + 1) * 2 * GROUP)
                y0, y1 = x0[:, lanes], x1[:, lanes]
                rows_m.append(jnp.where(first, y0, pltpu.roll(y1, GROUP, 1)))
                rows_m.append(jnp.where(first, pltpu.roll(y0, GROUP, 1), y1))
            turned = jnp.swapaxes(jnp.stack(rows_m), 0, 1)
            out_cols = slice(b * GROUP, (b + 2) * GROUP)
            for k in range(4):
                n = nblock // len(rows[k])
                for i, ref in enumerate(rows[k]):
                    cut = slice(i * n, (i + 1) * n)
                    field[k, cut, at, out_cols] = ref[:, at, out_cols] - turned[k * nblock + i * n:k * nblock + (i + 1) * n]
        for k in range(4):
            for i in range(2):
                to = (part * i if k < 2 else part * ((odd + i) % 2))
                store = pltpu.make_async_copy(field.at[k, pl.ds(i * part, part), pl.ds(c * step, step), :],
                                              out_ref.at[dp ^ k, pl.ds(to, part), pl.ds(c * step, step), :],
                                              sems.at[(c * 4 + k) * 2 + i])
                store.start()
                stores.append(store)
    for store in stores:
        store.wait()


def update_call(rows, *arrays):
    arrays = [r.reshape(-1, GROUP, COLS) for r in rows] + list(arrays)
    return pl.pallas_call(
        update_kernel,
        in_specs=[pl.BlockSpec(memory_space=pltpu.VMEM)] * len(arrays),
        out_specs=pl.BlockSpec(memory_space=pl.ANY),
        out_shape=jax.ShapeDtypeStruct((4, OWN // GROUP, GROUP, COLS), F32),
        scratch_shapes=[
            pltpu.VMEM((NB, 4, OWN // GROUP, BAND), F32),
            pltpu.VMEM((4, OWN // GROUP, GROUP, COLS), F32),
            pltpu.SemaphoreType.DMA((8 * GROUP // 8,)),
        ],
        compiler_params=pltpu.CompilerParams(vmem_limit_bytes=24 * 2**20),
        name="parameter_update",
    )(*[pltpu.with_memory_space_constraint(a, pltpu.VMEM) for a in arrays]).reshape(4 * OWN, COLS)


def local(grad_parts, momentum, params, band):
    band = band.astype(jnp.int32)
    vert = cosine_columns(band // GROUP)
    horiz = cosine_columns(band % GROUP)
    new_momentum, new_params = step_rows(grad_parts, momentum[0], params, vert, horiz)
    return (new_momentum[None], new_params)


def solution(mesh):
    return jax.shard_map(
        local,
        mesh=mesh,
        in_specs=(
            P("outer", "fsdp", "dp", None, None),
            P("outer", ("fsdp", "dp"), None),
            P(("fsdp", "dp"), None),
            P(),
        ),
        out_specs=(P("outer", ("fsdp", "dp"), None), P("fsdp", None)),
        check_vma=False,
    )
```

```python
import jax
import jax.numpy as jnp
from jax import lax
from jax.experimental import pallas as pl
from jax.experimental.pallas import tpu as pltpu
from jax.sharding import PartitionSpec as P

GROUP = 64
BAND = 256
COLS = 512
NB = COLS // GROUP
OWN = 512
ZROWS = 320
FIRST = 32
LANES = COLS // 128
AXES = ("fsdp", "dp", "outer")
beta = 0.9

F32 = jnp.float32
BF16 = jnp.bfloat16


def place(x, y, z, core):
    return z * 32 + ((y // 2) * 2 + core) * 8 + x * 2 + y % 2


def swap(value, x=0, y=0, z=0, core=0):
    pairs = []
    for px in range(4):
        for py in range(4):
            for pz in range(4):
                for pc in range(2):
                    pairs.append((place(px, py, pz, pc), place(px ^ x, py ^ y, (pz + z) % 4, pc ^ core)))
    return lax.ppermute(value, AXES, pairs)


def cosine_columns(freq):
    freq = freq.astype(F32)[None, :]
    pos = jnp.arange(GROUP, dtype=F32)[:, None]
    scale = jnp.where(freq == 0, jnp.sqrt(1.0 / GROUP), jnp.sqrt(2.0 / GROUP)).astype(F32)
    return scale * jnp.cos(jnp.pi * (2.0 * pos + 1.0) * freq / (2.0 * GROUP))


def split(value):
    high = value.astype(BF16)
    return high, (value - high.astype(F32)).astype(BF16)


def dot(a, b):
    return jnp.dot(a, b, preferred_element_type=F32)


def piece_source(step, z, yh, core, parts_ref):
    f, r, c, top, rows = step
    return parts_ref.at[(z + f) % 4, (yh + r) % 2, (core + c) % 2, pl.ds(top, rows), :]


def mark(z, piece, term, out):
    out[...] = jnp.zeros((8, 128), F32)


def piece_call(name, parts, steps, terms, after, outs, cost=1, result=False):
    outs = outs + [((8, 128), mark)]
    outs = [out if len(out) == 3 else out + (F32,) for out in outs]
    n_terms, n_after, n_outs, n_steps = len(terms), len(after), len(outs), len(steps)
    picked = [i for i, t in enumerate(terms) if isinstance(t, tuple)]

    def kernel(parts_ref, *refs):
        refs = list(refs)
        take = lambda n: [refs.pop(0) for _ in range(n)]
        term_refs, _, out_refs = take(n_terms), take(n_after), take(n_outs)
        bufs, held, sems = take(n_steps), take(len(picked)), take(n_steps + len(picked))
        z, dp, x = lax.axis_index("fsdp"), lax.axis_index("dp"), lax.axis_index("outer") // 2
        sources = [piece_source(s, z, dp // 2, dp % 2, parts_ref) for s in steps]
        sources += [terms[i][2](x, term_refs[i]) for i in picked]
        loads = []
        for src, buf, sem in zip(sources, bufs + held, sems):
            copy = pltpu.make_async_copy(src, buf, sem)
            copy.start()
            loads.append(copy)
        waiting = set(range(len(loads)))

        def loaded(i):
            if i in waiting:
                waiting.remove(i)
                loads[i].wait()
            return (bufs + held)[i]

        def term(i):
            return loaded(n_steps + picked.index(i)) if i in picked else term_refs[i]

        for (_, body, _), ref in zip(outs, out_refs):
            body(z, loaded, term, ref)
        for i in sorted(waiting):
            loads[i].wait()

    here, anywhere = pl.BlockSpec(memory_space=pltpu.VMEM), pl.BlockSpec(memory_space=pl.ANY)
    hold = lambda v: pltpu.with_memory_space_constraint(v, pltpu.VMEM)
    return pl.pallas_call(
        kernel,
        in_specs=[pl.BlockSpec(memory_space=pltpu.HBM)] + [anywhere if i in picked else here for i in range(n_terms)]
        + [anywhere] * n_after,
        out_specs=[here] * n_outs,
        out_shape=[(jax.ShapeDtypeStruct if result and i == 0 else pltpu.VMEM)(s, t) for i, (s, _, t) in enumerate(outs)],
        scratch_shapes=[pltpu.VMEM((s[4], COLS), BF16) for s in steps]
        + [pltpu.VMEM(terms[i][1], F32) for i in picked]
        + [pltpu.SemaphoreType.DMA] * (n_steps + len(picked)),
        compiler_params=pltpu.CompilerParams(vmem_limit_bytes=24 * 2**20),
        cost_estimate=pl.CostEstimate(flops=cost*100, bytes_accessed=cost, transcendentals=0),
        name=name,
    )(parts, *[t[0] if i in picked else hold(t) for i, t in enumerate(terms)], *after)


def encode(mom, vert, horiz):
    rows = mom.shape[0]
    w_high, w_low = split(horiz)
    x_high, x_low = split(mom)
    out = []
    for b in range(NB):
        cut = slice(b * GROUP, (b + 1) * GROUP)
        half = dot(x_high[:, cut], w_high) + dot(x_low[:, cut], w_high) + dot(x_high[:, cut], w_low)
        out.append(jnp.sum(half.reshape(rows // GROUP, GROUP, BAND) * vert[None], axis=1))
    return out


def step_rows(grad_parts, momentum, params, vert, horiz):
    parts = pltpu.with_memory_space_constraint(grad_parts.reshape(4, 2, 2, OWN, COLS), pltpu.HBM)
    vert_t, horiz_t = vert.T, horiz.T
    zr, yr, half = ZROWS, OWN - ZROWS, COLS // 2
    left, right = slice(0, half), slice(half, COLS)
    call = lambda name, *rest, **options: piece_call(name, parts, *rest, **options)
    up, down = (lambda v: swap(v, z=1)), (lambda v: swap(v, z=3))
    OPP, UP, DOWN, MINE = 2, 1, 3, 0

    def z_rows(f, r, c):
        return (f, r, c, 0, zr)

    def y_rows(f, r, c):
        return (f, r, c, zr, yr)

    def widen(name, groups, after, more=None):
        extra = 0 if more is None else more.shape[0]
        outs, first = [], 0
        for group in groups:
            tail = extra if group is groups[-1] else 0

            def body(z, piece, term, out, group=group, first=first, tail=tail):
                top = 0
                for i, step in enumerate(group):
                    out[top:top + step[4], :] = piece(first + i)[...].astype(F32)
                    top += step[4]
                if tail:
                    out[top:, :] = term(0)[...]

            outs.append(((sum(s[4] for s in group) + tail, COLS), body))
            first += len(group)
        return call(name, [s for group in groups for s in group], [] if more is None else [more], after, outs)

    def add(i_pieces, i_term, first, cols=slice(None), half_terms=(), full_terms=()):
        def run(z, piece, term, out):
            top = 0
            for i in i_pieces:
                n = piece(i).shape[0]
                cut = slice(top, top + n)
                value = term(i_term)[first + top:first + top + n, cols] + piece(i)[:, cols].astype(F32)
                for k in full_terms:
                    value = value + term(k)[cut, cols]
                for k in half_terms:
                    value = value + term(k)[cut]
                out[cut, :] = value
                top += n
        return run

    def side(i_pieces, i_term, first, h_add, i_add):
        def run(z, piece, term, out):
            for h, cols in enumerate((left, right)):
                body = add(i_pieces, i_term, first, cols, (i_add,) if h == h_add else ())
                body(z, piece, term, out.at[:, cols])
        return run

    w_first, ta = widen("widen_a", [[z_rows(OPP, 0, 1), z_rows(OPP, 1, 1), y_rows(OPP, 1, 1)]], [])
    c_first = swap(w_first, core=1)
    *w_b, tb = widen("widen_b", [
        [z_rows(UP, 0, 1), z_rows(UP, 1, 1)], [z_rows(DOWN, 0, 1), z_rows(DOWN, 1, 1)],
        [y_rows(UP, 1, 1), y_rows(DOWN, 1, 1), y_rows(MINE, 1, 1), y_rows(OPP, 0, 1)],
        [z_rows(MINE, 0, 1), z_rows(MINE, 1, 1)],
        [y_rows(UP, 0, 1), y_rows(DOWN, 0, 1), y_rows(MINE, 0, 1)]], [ta], params)
    c_up, c_down, c_cross, c_own, c_rest = [swap(w, core=1) for w in w_b]
    def params_part(top, n):
        def pick(x, ref):
            return ref.at[pl.ds(pl.multiple_of((x % 2) * (OWN // 2) + top, FIRST), n), :]
        return (params, (n, COLS), pick)

    def with_params(body, i_params):
        def run(z, piece, term, out):
            n = out.shape[0] - term(i_params).shape[0]
            body(z, piece, term, out.at[:n])
            out[n:, :] = term(i_params)[...]
        return run

    u1, d1, y1, t1 = call(
        "opposite", [z_rows(OPP, 0, 0), z_rows(OPP, 1, 0), y_rows(OPP, 1, 0)], [c_first, params_part(0, FIRST)], [tb],
        [((2 * zr, half), add((0, 1), 0, 0, left)), ((2 * zr, half), add((0, 1), 0, 0, right)),
         ((yr + FIRST, COLS), with_params(add((2,), 0, 2 * zr), 1))])
    gu1, gd1, gy1 = up(u1), down(d1), swap(y1, y=2)

    table_high, table_low, tt = call("band_table", [], [vert_t, horiz_t], [t1], band_table())
    fold = yr // 2

    def onward(i, first, h_add, i_add, cols):
        def run(z, piece, term, out):
            side((2 * i, 2 * i + 1), i, 0, h_add, i_add)(z, piece, term, out.at[:2 * zr])
            value = term(4)[3 * yr:, cols] + term(5)[:yr, cols] + piece(4)[:, cols].astype(F32)
            out[2 * zr:, left] = value[:fold]
            out[2 * zr:, right] = value[fold:]
        return run

    y2, _ = call(
        "crossing", [y_rows(UP, 1, 0), y_rows(DOWN, 1, 0), y_rows(MINE, 1, 0)],
        [c_cross, params_part(FIRST, OWN // 2 - FIRST)], [t1],
        [((3 * yr + OWN // 2 - FIRST, COLS), with_params(add((0, 1, 2), 0, 0), 1))])
    u2, d2, t2 = call(
        "sides", [z_rows(UP, 0, 0), z_rows(UP, 1, 0), z_rows(DOWN, 0, 0), z_rows(DOWN, 1, 0), y_rows(OPP, 0, 0)],
        [c_up, c_down, gu1, gd1, c_cross, gy1], [tt],
        [((2 * zr + fold, COLS), onward(0, 0, 0, 2, left)), ((2 * zr + fold, COLS), onward(1, 0, 1, 3, right))], cost=100000000)
    gu2, gd2, gy2 = up(u2), down(d2), swap(y2, y=2)

    def own_body(r):
        def run(z, piece, term, out):
            cut = slice(r * zr, (r + 1) * zr)
            out[...] = term(0)[cut] + piece(r)[...].astype(F32) + (term(1)[cut] + term(2)[cut])
        return run

    def last_side(i, h_add, i_add):
        def run(z, piece, term, out):
            cut = slice(i * yr, (i + 1) * yr)
            for h, cols in enumerate((left, right)):
                value = term(3)[cut, cols] + term(4)[cut, cols] + piece(2 + i)[:, cols].astype(F32)
                if h == h_add:
                    out[:fold, cols] = value[:fold] + term(i_add)[2 * zr:, left]
                    out[fold:, cols] = value[fold:] + term(i_add)[2 * zr:, right]
                else:
                    out[:, cols] = value
        return run

    def last_own_body(z, piece, term, out):
        out[...] = term(3)[2 * yr:3 * yr] + term(4)[2 * yr:3 * yr] + piece(4)[...].astype(F32)

    def far_body(z, piece, term, out):
        out[:FIRST, :] = term(5)[yr:, :]
        out[FIRST:, :] = term(3)[3 * yr:, :]

    far_rows, u4, d4, near, last_own, far_half, t6 = call(
        "own", [z_rows(MINE, 0, 0), z_rows(MINE, 1, 0), y_rows(UP, 0, 0), y_rows(DOWN, 0, 0), y_rows(MINE, 0, 0)],
        [c_own, gu2, gd2, gy2, c_rest, gy1], [t2],
        [((zr, COLS), own_body(1)), ((yr, COLS), last_side(0, 0, 1)), ((yr, COLS), last_side(1, 1, 2)),
         ((zr, COLS), own_body(0)), ((yr, COLS), last_own_body),
         ((OWN // 2, COLS), far_body)])
    far_other = swap(far_half, x=1)
    from_core = [swap(far_half, core=1)]
    gu4, gd4 = up(u4), down(d4)
    def momentum_rows(top, n):
        return (momentum, (n, COLS), lambda x, ref: ref.at[pl.ds(top, n), :])

    nz, ny = zr // GROUP, yr // GROUP

    def near_partial(z, piece, term, out):
        value = beta * term(2)[...] + term(0)[...] * (1.0 / 16.0)
        for b, (mine, theirs) in enumerate(zip(encode(value, term(3)[...], term(4)[...]),
                                               encode(term(1)[...] * (1.0 / 16.0), term(3)[...], term(4)[...]))):
            out[b, :nz, :] = mine
            out[b, nz:, :] = theirs

    def hand_on(z, piece, term, out):
        out[...] = term(1)[...]

    partial, y3, _ = call("partial_encode", [], [near, far_rows, momentum_rows(0, zr), vert, horiz], [t6],
                        [((NB, 2 * nz, BAND), near_partial), ((zr, COLS), hand_on)])
    gy3 = swap(y3, y=2)

    def last_mom(z, piece, term, out):
        grad = term(0)[...] + (term(1)[...] + term(2)[...])
        out[...] = beta * term(3)[...] + grad * (1.0 / 16.0)
        last_mom.value = out

    def last_coeffs(z, piece, term, out):
        for b, value in enumerate(encode(last_mom.value[...], term(4)[...], term(5)[...])):
            out[b, :nz, :] = term(6)[b, :nz]
            out[b, nz:nz + ny, :] = value
            out[b, nz + ny:, :] = term(6)[b, nz:]

    mom_low, coeffs, t7 = call(
        "last_momentum", [], [last_own, gu4, gd4, momentum_rows(zr, yr), vert, horiz, partial], [t6, far_other, from_core[0]],
        [((yr, COLS), last_mom), ((NB, 2 * nz + ny, BAND), last_coeffs)], cost=4 * 10**6,
    )

    def sum_four(z, piece, term, out):
        out[...] = (term(0)[...] + term(2)[...]) + (term(1)[...] + term(3)[...])

    total, tx = call("sum_x", [], [coeffs] + [swap(coeffs, x=k) for k in (2, 1, 3)], [], [(coeffs.shape, sum_four)],
                    cost=20000000)
    def near_mom(z, piece, term, out):
        out[...] = beta * term(2)[...] + (term(0)[...] + term(1)[...]) * (1.0 / 16.0)
        near_mom.value = out

    def near_shared(z, piece, term, out):
        for b, value in enumerate(encode(near_mom.value[...], term(3)[...], term(4)[...])):
            out[b, :nz, :] = value
            out[b, nz:, :] = term(5)[b, nz:nz + ny]

    def far_copy(z, piece, term, out):
        out[...] = term(6)[...]

    mom_top, shared, far_late, t8 = call(
        "near_momentum", [], [near, gy3, momentum_rows(0, zr), vert, horiz, coeffs, far_other], [tx],
        [((zr, COLS), near_mom), ((NB, nz + ny, BAND), near_shared), ((OWN // 2, COLS), far_copy)], cost=5 * 10**6,
    )
    from_core.append(swap(far_late, core=1))

    def residual(z, piece, term, out):
        high, low = split(term(4)[...])
        w_both = jnp.concatenate([high, low], axis=1)
        vert_now = term(3)[...][None]
        for pair in range(NB // 2):
            sides = []
            for b in (2 * pair, 2 * pair + 1):
                wide = (term(2)[b][:, None, :] * vert_now).reshape(OWN, BAND)
                wide_high, wide_low = split(wide)
                both = dot(wide_high, w_both)
                sides.append(both[:, :GROUP] + both[:, GROUP:] + dot(wide_low, w_both[:, :GROUP]))
            cols = slice(pair * 2 * GROUP, (pair + 1) * 2 * GROUP)
            value = jnp.concatenate(sides, axis=1)
            out[:zr, cols] = term(0)[:, cols] - value[:zr]
            out[zr:, cols] = term(1)[:, cols] - value[zr:]

    new_momentum, t9 = call("momentum_residual", [], [mom_top, mom_low, shared, vert, horiz_t], [t8],
                            [((OWN, COLS), residual)], cost=9 * 10**6, result=True)

    def sum_pairs(z, piece, term, out):
        top, low, far = slice(0, nz), slice(nz, nz + ny), slice(nz + ny, None)
        for k, (a, b, c, d) in enumerate(((0, 2, 1, 3), (1, 3, 0, 2))):
            own = [term(a)[:, cut] + term(b)[:, cut] for cut in (top, low)]
            out[k, :, :nz, :] = own[0] + (term(c)[:, far] + term(d)[:, far])
            out[k, :, nz:, :] = own[1]

    pair, _ = call("sum_y", [], [total] + [swap(total, y=k) for k in (2, 1, 3)], [t9], [((2,) + shared.shape, sum_pairs)],
                   cost=7 * 10**7)
    new_params = update_call([params, far_half, far_other, c_rest] + from_core, pair, swap(pair, core=1), table_high, table_low)
    return new_momentum, new_params


def band_table():
    held = {}

    def high(z, piece, term, out):
        lane = lax.broadcasted_iota(jnp.int32, (BAND, 2 * GROUP), 1)
        horiz = jnp.concatenate([term(1)[...]] * 2, axis=1)
        vert = term(0)[...]
        held["low"] = []
        for m in range(0, GROUP, 2):
            product = jnp.where(lane < GROUP, vert[:, m:m + 1], vert[:, m + 1:m + 2]) * horiz
            top, rest = split(product)
            out[:, m * GROUP:(m + 2) * GROUP] = top
            held["low"].append(rest)

    def low(z, piece, term, out):
        for i, rest in enumerate(held["low"]):
            out[:, 2 * i * GROUP:2 * (i + 1) * GROUP] = rest

    return [((BAND, GROUP * GROUP), high, BF16), ((BAND, GROUP * GROUP), low, BF16)]


def update_kernel(own_ref, far_ref, other_ref, core_own_ref, core_far_ref, core_other_ref,
                  pair_ref, pair_core_ref, high_ref, low_ref, out_ref, coeff, field, sems):
    dp = lax.axis_index("dp")
    odd = (lax.axis_index("outer") // 2) % 2
    nblock = OWN // GROUP
    part = nblock // 2
    core_own = core_own_ref.at[core_own_ref.shape[0] - nblock:]
    rows = ((own_ref,), (core_own,), (far_ref, other_ref), (core_far_ref, core_other_ref))
    for k in range(4):
        value = (pair_ref, pair_core_ref)[k % 2][k // 2]
        if k >= 2:
            turned = jnp.concatenate([value[:, part:], value[:, :part]], axis=1)
            value = jnp.where(odd == 1, turned, value)
        coeff[:, k] = value
    c_high, c_low = split(coeff[...].reshape(NB * 4 * nblock, BAND) * (1.0 / 8.0))
    both = jnp.concatenate([c_high, c_low], axis=0)
    lane = lax.broadcasted_iota(jnp.int32, (4 * nblock, 2 * GROUP), 1)
    first = lane < GROUP
    step = 8
    stores = []
    for c in range(GROUP // step):
        cols = slice(c * step * GROUP, (c + 1) * step * GROUP)
        wide = dot(both, high_ref[:, cols])
        value = wide[:NB * 4 * nblock] + wide[NB * 4 * nblock:] + dot(c_high, low_ref[:, cols])
        at = slice(c * step, (c + 1) * step)
        for b in range(0, NB, 2):
            x0, x1 = [value[i * 4 * nblock:(i + 1) * 4 * nblock] for i in (b, b + 1)]
            rows_m = []
            for lt in range(step // 2):
                lanes = slice(lt * 2 * GROUP, (lt + 1) * 2 * GROUP)
                y0, y1 = x0[:, lanes], x1[:, lanes]
                rows_m.append(jnp.where(first, y0, pltpu.roll(y1, GROUP, 1)))
                rows_m.append(jnp.where(first, pltpu.roll(y0, GROUP, 1), y1))
            turned = jnp.swapaxes(jnp.stack(rows_m), 0, 1)
            out_cols = slice(b * GROUP, (b + 2) * GROUP)
            for k in range(4):
                n = nblock // len(rows[k])
                for i, ref in enumerate(rows[k]):
                    cut = slice(i * n, (i + 1) * n)
                    field[k, cut, at, out_cols] = ref[:, at, out_cols] - turned[k * nblock + i * n:k * nblock + (i + 1) * n]
        for k in range(4):
            for i in range(2):
                to = (part * i if k < 2 else part * ((odd + i) % 2))
                store = pltpu.make_async_copy(field.at[k, pl.ds(i * part, part), pl.ds(c * step, step), :],
                                              out_ref.at[dp ^ k, pl.ds(to, part), pl.ds(c * step, step), :],
                                              sems.at[(c * 4 + k) * 2 + i])
                store.start()
                stores.append(store)
    for store in stores:
        store.wait()


def update_call(rows, *arrays):
    arrays = [r.reshape(-1, GROUP, COLS) for r in rows] + list(arrays)
    return pl.pallas_call(
        update_kernel,
        in_specs=[pl.BlockSpec(memory_space=pltpu.VMEM)] * len(arrays),
        out_specs=pl.BlockSpec(memory_space=pl.ANY),
        out_shape=jax.ShapeDtypeStruct((4, OWN // GROUP, GROUP, COLS), F32),
        scratch_shapes=[
            pltpu.VMEM((NB, 4, OWN // GROUP, BAND), F32),
            pltpu.VMEM((4, OWN // GROUP, GROUP, COLS), F32),
            pltpu.SemaphoreType.DMA((8 * GROUP // 8,)),
        ],
        compiler_params=pltpu.CompilerParams(vmem_limit_bytes=24 * 2**20),
        name="parameter_update",
    )(*[pltpu.with_memory_space_constraint(a, pltpu.VMEM) for a in arrays]).reshape(4 * OWN, COLS)


def local(grad_parts, momentum, params, band):
    band = band.astype(jnp.int32)
    vert = cosine_columns(band // GROUP)
    horiz = cosine_columns(band % GROUP)
    new_momentum, new_params = step_rows(grad_parts, momentum[0], params, vert, horiz)
    return (new_momentum[None], new_params)


def solution(mesh):
    return jax.shard_map(
        local,
        mesh=mesh,
        in_specs=(
            P("outer", "fsdp", "dp", None, None),
            P("outer", ("fsdp", "dp"), None),
            P(("fsdp", "dp"), None),
            P(),
        ),
        out_specs=(P("outer", ("fsdp", "dp"), None), P("fsdp", None)),
        check_vma=False,
    )
```

```python
import jax
import jax.numpy as jnp
from jax import lax
from jax.experimental import pallas as pl
from jax.experimental.pallas import tpu as pltpu
from jax.sharding import PartitionSpec as P

GROUP = 64
BAND = 256
COLS = 512
NB = COLS // GROUP
OWN = 512
ZROWS = 320
FIRST = 32
LANES = COLS // 128
AXES = ("fsdp", "dp", "outer")
beta = 0.9

F32 = jnp.float32
BF16 = jnp.bfloat16


def place(x, y, z, core):
    return z * 32 + ((y // 2) * 2 + core) * 8 + x * 2 + y % 2


def swap(value, x=0, y=0, z=0, core=0):
    pairs = []
    for px in range(4):
        for py in range(4):
            for pz in range(4):
                for pc in range(2):
                    pairs.append((place(px, py, pz, pc), place(px ^ x, py ^ y, (pz + z) % 4, pc ^ core)))
    return lax.ppermute(value, AXES, pairs)


def cosine_columns(freq):
    freq = freq.astype(F32)[None, :]
    pos = jnp.arange(GROUP, dtype=F32)[:, None]
    scale = jnp.where(freq == 0, jnp.sqrt(1.0 / GROUP), jnp.sqrt(2.0 / GROUP)).astype(F32)
    return scale * jnp.cos(jnp.pi * (2.0 * pos + 1.0) * freq / (2.0 * GROUP))


def split(value):
    high = value.astype(BF16)
    return high, (value - high.astype(F32)).astype(BF16)


def dot(a, b):
    return jnp.dot(a, b, preferred_element_type=F32)


def piece_source(step, z, yh, core, parts_ref):
    f, r, c, top, rows = step
    return parts_ref.at[(z + f) % 4, (yh + r) % 2, (core + c) % 2, pl.ds(top, rows), :]


def mark(z, piece, term, out):
    out[...] = jnp.zeros((8, 128), F32)


def piece_call(name, parts, steps, terms, after, outs, cost=1, result=False):
    outs = outs + [((8, 128), mark)]
    outs = [out if len(out) == 3 else out + (F32,) for out in outs]
    n_terms, n_after, n_outs, n_steps = len(terms), len(after), len(outs), len(steps)
    picked = [i for i, t in enumerate(terms) if isinstance(t, tuple)]

    def kernel(parts_ref, *refs):
        refs = list(refs)
        take = lambda n: [refs.pop(0) for _ in range(n)]
        term_refs, _, out_refs = take(n_terms), take(n_after), take(n_outs)
        bufs, held, sems = take(n_steps), take(len(picked)), take(n_steps + len(picked))
        z, dp, x = lax.axis_index("fsdp"), lax.axis_index("dp"), lax.axis_index("outer") // 2
        sources = [piece_source(s, z, dp // 2, dp % 2, parts_ref) for s in steps]
        sources += [terms[i][2](x, term_refs[i]) for i in picked]
        loads = []
        for src, buf, sem in zip(sources, bufs + held, sems):
            copy = pltpu.make_async_copy(src, buf, sem)
            copy.start()
            loads.append(copy)
        waiting = set(range(len(loads)))

        def loaded(i):
            if i in waiting:
                waiting.remove(i)
                loads[i].wait()
            return (bufs + held)[i]

        def term(i):
            return loaded(n_steps + picked.index(i)) if i in picked else term_refs[i]

        for (_, body, _), ref in zip(outs, out_refs):
            body(z, loaded, term, ref)
        for i in sorted(waiting):
            loads[i].wait()

    here, anywhere = pl.BlockSpec(memory_space=pltpu.VMEM), pl.BlockSpec(memory_space=pl.ANY)
    hold = lambda v: pltpu.with_memory_space_constraint(v, pltpu.VMEM)
    return pl.pallas_call(
        kernel,
        in_specs=[pl.BlockSpec(memory_space=pltpu.HBM)] + [anywhere if i in picked else here for i in range(n_terms)]
        + [anywhere] * n_after,
        out_specs=[here] * n_outs,
        out_shape=[(jax.ShapeDtypeStruct if result and i == 0 else pltpu.VMEM)(s, t) for i, (s, _, t) in enumerate(outs)],
        scratch_shapes=[pltpu.VMEM((s[4], COLS), BF16) for s in steps]
        + [pltpu.VMEM(terms[i][1], F32) for i in picked]
        + [pltpu.SemaphoreType.DMA] * (n_steps + len(picked)),
        compiler_params=pltpu.CompilerParams(vmem_limit_bytes=24 * 2**20),
        cost_estimate=pl.CostEstimate(flops=cost*100, bytes_accessed=cost, transcendentals=0),
        name=name,
    )(parts, *[t[0] if i in picked else hold(t) for i, t in enumerate(terms)], *after)


def encode(mom, vert, horiz):
    rows = mom.shape[0]
    w_high, w_low = split(horiz)
    x_high, x_low = split(mom)
    out = []
    for b in range(NB):
        cut = slice(b * GROUP, (b + 1) * GROUP)
        half = dot(x_high[:, cut], w_high) + dot(x_low[:, cut], w_high) + dot(x_high[:, cut], w_low)
        out.append(jnp.sum(half.reshape(rows // GROUP, GROUP, BAND) * vert[None], axis=1))
    return out


def step_rows(grad_parts, momentum, params, vert, horiz):
    parts = pltpu.with_memory_space_constraint(grad_parts.reshape(4, 2, 2, OWN, COLS), pltpu.HBM)
    vert_t, horiz_t = vert.T, horiz.T
    zr, yr, half = ZROWS, OWN - ZROWS, COLS // 2
    left, right = slice(0, half), slice(half, COLS)
    call = lambda name, *rest, **options: piece_call(name, parts, *rest, **options)
    up, down = (lambda v: swap(v, z=1)), (lambda v: swap(v, z=3))
    OPP, UP, DOWN, MINE = 2, 1, 3, 0

    def z_rows(f, r, c):
        return (f, r, c, 0, zr)

    def y_rows(f, r, c):
        return (f, r, c, zr, yr)

    def widen(name, groups, after, more=None):
        extra = 0 if more is None else more.shape[0]
        outs, first = [], 0
        for group in groups:
            tail = extra if group is groups[-1] else 0

            def body(z, piece, term, out, group=group, first=first, tail=tail):
                top = 0
                for i, step in enumerate(group):
                    out[top:top + step[4], :] = piece(first + i)[...].astype(F32)
                    top += step[4]
                if tail:
                    out[top:, :] = term(0)[...]

            outs.append(((sum(s[4] for s in group) + tail, COLS), body))
            first += len(group)
        return call(name, [s for group in groups for s in group], [] if more is None else [more], after, outs)

    def add(i_pieces, i_term, first, cols=slice(None), half_terms=(), full_terms=()):
        def run(z, piece, term, out):
            top = 0
            for i in i_pieces:
                n = piece(i).shape[0]
                cut = slice(top, top + n)
                value = term(i_term)[first + top:first + top + n, cols] + piece(i)[:, cols].astype(F32)
                for k in full_terms:
                    value = value + term(k)[cut, cols]
                for k in half_terms:
                    value = value + term(k)[cut]
                out[cut, :] = value
                top += n
        return run

    def side(i_pieces, i_term, first, h_add, i_add):
        def run(z, piece, term, out):
            for h, cols in enumerate((left, right)):
                body = add(i_pieces, i_term, first, cols, (i_add,) if h == h_add else ())
                body(z, piece, term, out.at[:, cols])
        return run

    w_first, ta = widen("widen_a", [[z_rows(OPP, 0, 1), z_rows(OPP, 1, 1), y_rows(OPP, 1, 1)]], [])
    c_first = swap(w_first, core=1)
    *w_b, tb = widen("widen_b", [
        [z_rows(UP, 0, 1), z_rows(UP, 1, 1)], [z_rows(DOWN, 0, 1), z_rows(DOWN, 1, 1)],
        [y_rows(UP, 1, 1), y_rows(DOWN, 1, 1), y_rows(MINE, 1, 1), y_rows(OPP, 0, 1)],
        [z_rows(MINE, 0, 1), z_rows(MINE, 1, 1)],
        [y_rows(UP, 0, 1), y_rows(DOWN, 0, 1), y_rows(MINE, 0, 1)]], [ta], params)
    c_up, c_down, c_cross, c_own, c_rest = [swap(w, core=1) for w in w_b]
    def params_part(top, n):
        def pick(x, ref):
            return ref.at[pl.ds(pl.multiple_of((x % 2) * (OWN // 2) + top, FIRST), n), :]
        return (params, (n, COLS), pick)

    def with_params(body, i_params):
        def run(z, piece, term, out):
            n = out.shape[0] - term(i_params).shape[0]
            body(z, piece, term, out.at[:n])
            out[n:, :] = term(i_params)[...]
        return run

    u1, d1, y1, t1 = call(
        "opposite", [z_rows(OPP, 0, 0), z_rows(OPP, 1, 0), y_rows(OPP, 1, 0)], [c_first, params_part(0, FIRST)], [tb],
        [((2 * zr, half), add((0, 1), 0, 0, left)), ((2 * zr, half), add((0, 1), 0, 0, right)),
         ((yr + FIRST, COLS), with_params(add((2,), 0, 2 * zr), 1))])
    gu1, gd1, gy1 = up(u1), down(d1), swap(y1, y=2)

    table_high, table_low, tt = call("band_table", [], [vert_t, horiz_t], [t1], band_table())
    fold = yr // 2

    def onward(i, first, h_add, i_add, cols):
        def run(z, piece, term, out):
            side((2 * i, 2 * i + 1), i, 0, h_add, i_add)(z, piece, term, out.at[:2 * zr])
            value = term(4)[3 * yr:, cols] + term(5)[:yr, cols] + piece(4)[:, cols].astype(F32)
            out[2 * zr:, left] = value[:fold]
            out[2 * zr:, right] = value[fold:]
        return run

    y2, _ = call(
        "crossing", [y_rows(UP, 1, 0), y_rows(DOWN, 1, 0), y_rows(MINE, 1, 0)],
        [c_cross, params_part(FIRST, OWN // 2 - FIRST)], [t1],
        [((3 * yr + OWN // 2 - FIRST, COLS), with_params(add((0, 1, 2), 0, 0), 1))])
    u2, d2, t2 = call(
        "sides", [z_rows(UP, 0, 0), z_rows(UP, 1, 0), z_rows(DOWN, 0, 0), z_rows(DOWN, 1, 0), y_rows(OPP, 0, 0)],
        [c_up, c_down, gu1, gd1, c_cross, gy1], [tt],
        [((2 * zr + fold, COLS), onward(0, 0, 0, 2, left)), ((2 * zr + fold, COLS), onward(1, 0, 1, 3, right))], cost=100000000)
    gu2, gd2, gy2 = up(u2), down(d2), swap(y2, y=2)

    def own_body(r):
        def run(z, piece, term, out):
            cut = slice(r * zr, (r + 1) * zr)
            out[...] = term(0)[cut] + piece(r)[...].astype(F32) + (term(1)[cut] + term(2)[cut])
        return run

    def last_side(i, h_add, i_add):
        def run(z, piece, term, out):
            cut = slice(i * yr, (i + 1) * yr)
            for h, cols in enumerate((left, right)):
                value = term(3)[cut, cols] + term(4)[cut, cols] + piece(2 + i)[:, cols].astype(F32)
                if h == h_add:
                    out[:fold, cols] = value[:fold] + term(i_add)[2 * zr:, left]
                    out[fold:, cols] = value[fold:] + term(i_add)[2 * zr:, right]
                else:
                    out[:, cols] = value
        return run

    def last_own_body(z, piece, term, out):
        out[...] = term(3)[2 * yr:3 * yr] + term(4)[2 * yr:3 * yr] + piece(4)[...].astype(F32)

    def far_body(z, piece, term, out):
        out[:FIRST, :] = term(0)[yr:, :]
        out[FIRST:, :] = term(1)[3 * yr:, :]

    far_half, tf = call("far_rows", [], [gy1, gy2], [t2], [((OWN // 2, COLS), far_body)], cost=1)
    far_rows, u4, d4, near, last_own, t6 = call(
        "own", [z_rows(MINE, 0, 0), z_rows(MINE, 1, 0), y_rows(UP, 0, 0), y_rows(DOWN, 0, 0), y_rows(MINE, 0, 0)],
        [c_own, gu2, gd2, gy2, c_rest], [tf],
        [((zr, COLS), own_body(1)), ((yr, COLS), last_side(0, 0, 1)), ((yr, COLS), last_side(1, 1, 2)),
         ((zr, COLS), own_body(0)), ((yr, COLS), last_own_body)])
    far_other = swap(far_half, x=1)
    from_core = [swap(far_half, core=1)]
    gu4, gd4 = up(u4), down(d4)
    def momentum_rows(top, n):
        return (momentum, (n, COLS), lambda x, ref: ref.at[pl.ds(top, n), :])

    nz, ny = zr // GROUP, yr // GROUP

    def near_partial(z, piece, term, out):
        value = beta * term(2)[...] + term(0)[...] * (1.0 / 16.0)
        for b, (mine, theirs) in enumerate(zip(encode(value, term(3)[...], term(4)[...]),
                                               encode(term(1)[...] * (1.0 / 16.0), term(3)[...], term(4)[...]))):
            out[b, :nz, :] = mine
            out[b, nz:, :] = theirs

    def hand_on(z, piece, term, out):
        out[...] = term(1)[...]

    partial, y3, _ = call("partial_encode", [], [near, far_rows, momentum_rows(0, zr), vert, horiz], [t6],
                        [((NB, 2 * nz, BAND), near_partial), ((zr, COLS), hand_on)])
    gy3 = swap(y3, y=2)

    def last_mom(z, piece, term, out):
        grad = term(0)[...] + (term(1)[...] + term(2)[...])
        out[...] = beta * term(3)[...] + grad * (1.0 / 16.0)
        last_mom.value = out

    def last_coeffs(z, piece, term, out):
        for b, value in enumerate(encode(last_mom.value[...], term(4)[...], term(5)[...])):
            out[b, :nz, :] = term(6)[b, :nz]
            out[b, nz:nz + ny, :] = value
            out[b, nz + ny:, :] = term(6)[b, nz:]

    mom_low, coeffs, t7 = call(
        "last_momentum", [], [last_own, gu4, gd4, momentum_rows(zr, yr), vert, horiz, partial], [t6, far_other, from_core[0]],
        [((yr, COLS), last_mom), ((NB, 2 * nz + ny, BAND), last_coeffs)], cost=4 * 10**6,
    )

    def sum_four(z, piece, term, out):
        out[...] = (term(0)[...] + term(2)[...]) + (term(1)[...] + term(3)[...])

    total, tx = call("sum_x", [], [coeffs] + [swap(coeffs, x=k) for k in (2, 1, 3)], [], [(coeffs.shape, sum_four)],
                    cost=20000000)
    def near_mom(z, piece, term, out):
        out[...] = beta * term(2)[...] + (term(0)[...] + term(1)[...]) * (1.0 / 16.0)
        near_mom.value = out

    def near_shared(z, piece, term, out):
        for b, value in enumerate(encode(near_mom.value[...], term(3)[...], term(4)[...])):
            out[b, :nz, :] = value
            out[b, nz:, :] = term(5)[b, nz:nz + ny]

    def far_copy(z, piece, term, out):
        out[...] = term(6)[...]

    mom_top, shared, far_late, t8 = call(
        "near_momentum", [], [near, gy3, momentum_rows(0, zr), vert, horiz, coeffs, far_other], [tx],
        [((zr, COLS), near_mom), ((NB, nz + ny, BAND), near_shared), ((OWN // 2, COLS), far_copy)], cost=5 * 10**6,
    )
    from_core.append(swap(far_late, core=1))

    def residual(z, piece, term, out):
        high, low = split(term(4)[...])
        w_both = jnp.concatenate([high, low], axis=1)
        vert_now = term(3)[...][None]
        for pair in range(NB // 2):
            sides = []
            for b in (2 * pair, 2 * pair + 1):
                wide = (term(2)[b][:, None, :] * vert_now).reshape(OWN, BAND)
                wide_high, wide_low = split(wide)
                both = dot(wide_high, w_both)
                sides.append(both[:, :GROUP] + both[:, GROUP:] + dot(wide_low, w_both[:, :GROUP]))
            cols = slice(pair * 2 * GROUP, (pair + 1) * 2 * GROUP)
            value = jnp.concatenate(sides, axis=1)
            out[:zr, cols] = term(0)[:, cols] - value[:zr]
            out[zr:, cols] = term(1)[:, cols] - value[zr:]

    new_momentum, t9 = call("momentum_residual", [], [mom_top, mom_low, shared, vert, horiz_t], [t8],
                            [((OWN, COLS), residual)], cost=9 * 10**6, result=True)

    def sum_pairs(z, piece, term, out):
        top, low, far = slice(0, nz), slice(nz, nz + ny), slice(nz + ny, None)
        for k, (a, b, c, d) in enumerate(((0, 2, 1, 3), (1, 3, 0, 2))):
            own = [term(a)[:, cut] + term(b)[:, cut] for cut in (top, low)]
            out[k, :, :nz, :] = own[0] + (term(c)[:, far] + term(d)[:, far])
            out[k, :, nz:, :] = own[1]

    pair, _ = call("sum_y", [], [total] + [swap(total, y=k) for k in (2, 1, 3)], [t9], [((2,) + shared.shape, sum_pairs)],
                   cost=7 * 10**7)
    new_params = update_call([params, far_half, far_other, c_rest] + from_core, pair, swap(pair, core=1), table_high, table_low)
    return new_momentum, new_params


def band_table():
    held = {}

    def high(z, piece, term, out):
        lane = lax.broadcasted_iota(jnp.int32, (BAND, 2 * GROUP), 1)
        horiz = jnp.concatenate([term(1)[...]] * 2, axis=1)
        vert = term(0)[...]
        held["low"] = []
        for m in range(0, GROUP, 2):
            product = jnp.where(lane < GROUP, vert[:, m:m + 1], vert[:, m + 1:m + 2]) * horiz
            top, rest = split(product)
            out[:, m * GROUP:(m + 2) * GROUP] = top
            held["low"].append(rest)

    def low(z, piece, term, out):
        for i, rest in enumerate(held["low"]):
            out[:, 2 * i * GROUP:2 * (i + 1) * GROUP] = rest

    return [((BAND, GROUP * GROUP), high, BF16), ((BAND, GROUP * GROUP), low, BF16)]


def update_kernel(own_ref, far_ref, other_ref, core_own_ref, core_far_ref, core_other_ref,
                  pair_ref, pair_core_ref, high_ref, low_ref, out_ref, coeff, field, sems):
    dp = lax.axis_index("dp")
    odd = (lax.axis_index("outer") // 2) % 2
    nblock = OWN // GROUP
    part = nblock // 2
    core_own = core_own_ref.at[core_own_ref.shape[0] - nblock:]
    rows = ((own_ref,), (core_own,), (far_ref, other_ref), (core_far_ref, core_other_ref))
    for k in range(4):
        value = (pair_ref, pair_core_ref)[k % 2][k // 2]
        if k >= 2:
            turned = jnp.concatenate([value[:, part:], value[:, :part]], axis=1)
            value = jnp.where(odd == 1, turned, value)
        coeff[:, k] = value
    c_high, c_low = split(coeff[...].reshape(NB * 4 * nblock, BAND) * (1.0 / 8.0))
    both = jnp.concatenate([c_high, c_low], axis=0)
    lane = lax.broadcasted_iota(jnp.int32, (4 * nblock, 2 * GROUP), 1)
    first = lane < GROUP
    step = 8
    stores = []
    for c in range(GROUP // step):
        cols = slice(c * step * GROUP, (c + 1) * step * GROUP)
        wide = dot(both, high_ref[:, cols])
        value = wide[:NB * 4 * nblock] + wide[NB * 4 * nblock:] + dot(c_high, low_ref[:, cols])
        at = slice(c * step, (c + 1) * step)
        for b in range(0, NB, 2):
            x0, x1 = [value[i * 4 * nblock:(i + 1) * 4 * nblock] for i in (b, b + 1)]
            rows_m = []
            for lt in range(step // 2):
                lanes = slice(lt * 2 * GROUP, (lt + 1) * 2 * GROUP)
                y0, y1 = x0[:, lanes], x1[:, lanes]
                rows_m.append(jnp.where(first, y0, pltpu.roll(y1, GROUP, 1)))
                rows_m.append(jnp.where(first, pltpu.roll(y0, GROUP, 1), y1))
            turned = jnp.swapaxes(jnp.stack(rows_m), 0, 1)
            out_cols = slice(b * GROUP, (b + 2) * GROUP)
            for k in range(4):
                n = nblock // len(rows[k])
                for i, ref in enumerate(rows[k]):
                    cut = slice(i * n, (i + 1) * n)
                    field[k, cut, at, out_cols] = ref[:, at, out_cols] - turned[k * nblock + i * n:k * nblock + (i + 1) * n]
        for k in range(4):
            for i in range(2):
                to = (part * i if k < 2 else part * ((odd + i) % 2))
                store = pltpu.make_async_copy(field.at[k, pl.ds(i * part, part), pl.ds(c * step, step), :],
                                              out_ref.at[dp ^ k, pl.ds(to, part), pl.ds(c * step, step), :],
                                              sems.at[(c * 4 + k) * 2 + i])
                store.start()
                stores.append(store)
    for store in stores:
        store.wait()


def update_call(rows, *arrays):
    arrays = [r.reshape(-1, GROUP, COLS) for r in rows] + list(arrays)
    return pl.pallas_call(
        update_kernel,
        in_specs=[pl.BlockSpec(memory_space=pltpu.VMEM)] * len(arrays),
        out_specs=pl.BlockSpec(memory_space=pl.ANY),
        out_shape=jax.ShapeDtypeStruct((4, OWN // GROUP, GROUP, COLS), F32),
        scratch_shapes=[
            pltpu.VMEM((NB, 4, OWN // GROUP, BAND), F32),
            pltpu.VMEM((4, OWN // GROUP, GROUP, COLS), F32),
            pltpu.SemaphoreType.DMA((8 * GROUP // 8,)),
        ],
        compiler_params=pltpu.CompilerParams(vmem_limit_bytes=24 * 2**20),
        name="parameter_update",
    )(*[pltpu.with_memory_space_constraint(a, pltpu.VMEM) for a in arrays]).reshape(4 * OWN, COLS)


def local(grad_parts, momentum, params, band):
    band = band.astype(jnp.int32)
    vert = cosine_columns(band // GROUP)
    horiz = cosine_columns(band % GROUP)
    new_momentum, new_params = step_rows(grad_parts, momentum[0], params, vert, horiz)
    return (new_momentum[None], new_params)


def solution(mesh):
    return jax.shard_map(
        local,
        mesh=mesh,
        in_specs=(
            P("outer", "fsdp", "dp", None, None),
            P("outer", ("fsdp", "dp"), None),
            P(("fsdp", "dp"), None),
            P(),
        ),
        out_specs=(P("outer", ("fsdp", "dp"), None), P("fsdp", None)),
        check_vma=False,
    )
```

```python
import jax
import jax.numpy as jnp
from jax import lax
from jax.experimental import pallas as pl
from jax.experimental.pallas import tpu as pltpu
from jax.sharding import PartitionSpec as P

GROUP = 64
BAND = 256
COLS = 512
NB = COLS // GROUP
OWN = 512
ZROWS = 320
FIRST = 32
LANES = COLS // 128
AXES = ("fsdp", "dp", "outer")
beta = 0.9

F32 = jnp.float32
BF16 = jnp.bfloat16


def place(x, y, z, core):
    return z * 32 + ((y // 2) * 2 + core) * 8 + x * 2 + y % 2


def swap(value, x=0, y=0, z=0, core=0):
    pairs = []
    for px in range(4):
        for py in range(4):
            for pz in range(4):
                for pc in range(2):
                    pairs.append((place(px, py, pz, pc), place(px ^ x, py ^ y, (pz + z) % 4, pc ^ core)))
    return lax.ppermute(value, AXES, pairs)


def cosine_columns(freq):
    freq = freq.astype(F32)[None, :]
    pos = jnp.arange(GROUP, dtype=F32)[:, None]
    scale = jnp.where(freq == 0, jnp.sqrt(1.0 / GROUP), jnp.sqrt(2.0 / GROUP)).astype(F32)
    return scale * jnp.cos(jnp.pi * (2.0 * pos + 1.0) * freq / (2.0 * GROUP))


def split(value):
    high = value.astype(BF16)
    return high, (value - high.astype(F32)).astype(BF16)


def dot(a, b):
    return jnp.dot(a, b, preferred_element_type=F32)


def piece_source(step, z, yh, core, parts_ref):
    f, r, c, top, rows = step
    return parts_ref.at[(z + f) % 4, (yh + r) % 2, (core + c) % 2, pl.ds(top, rows), :]


def mark(z, piece, term, out):
    out[...] = jnp.zeros((8, 128), F32)


def piece_call(name, parts, steps, terms, after, outs, cost=1, result=False):
    outs = outs + [((8, 128), mark)]
    outs = [out if len(out) == 3 else out + (F32,) for out in outs]
    n_terms, n_after, n_outs, n_steps = len(terms), len(after), len(outs), len(steps)
    picked = [i for i, t in enumerate(terms) if isinstance(t, tuple)]

    def kernel(parts_ref, *refs):
        refs = list(refs)
        take = lambda n: [refs.pop(0) for _ in range(n)]
        term_refs, _, out_refs = take(n_terms), take(n_after), take(n_outs)
        bufs, held, sems = take(n_steps), take(len(picked)), take(n_steps + len(picked))
        z, dp, x = lax.axis_index("fsdp"), lax.axis_index("dp"), lax.axis_index("outer") // 2
        sources = [piece_source(s, z, dp // 2, dp % 2, parts_ref) for s in steps]
        sources += [terms[i][2](x, term_refs[i]) for i in picked]
        loads = []
        for src, buf, sem in zip(sources, bufs + held, sems):
            copy = pltpu.make_async_copy(src, buf, sem)
            copy.start()
            loads.append(copy)
        waiting = set(range(len(loads)))

        def loaded(i):
            if i in waiting:
                waiting.remove(i)
                loads[i].wait()
            return (bufs + held)[i]

        def term(i):
            return loaded(n_steps + picked.index(i)) if i in picked else term_refs[i]

        for (_, body, _), ref in zip(outs, out_refs):
            body(z, loaded, term, ref)
        for i in sorted(waiting):
            loads[i].wait()

    here, anywhere = pl.BlockSpec(memory_space=pltpu.VMEM), pl.BlockSpec(memory_space=pl.ANY)
    hold = lambda v: pltpu.with_memory_space_constraint(v, pltpu.VMEM)
    return pl.pallas_call(
        kernel,
        in_specs=[pl.BlockSpec(memory_space=pltpu.HBM)] + [anywhere if i in picked else here for i in range(n_terms)]
        + [anywhere] * n_after,
        out_specs=[here] * n_outs,
        out_shape=[(jax.ShapeDtypeStruct if result and i == 0 else pltpu.VMEM)(s, t) for i, (s, _, t) in enumerate(outs)],
        scratch_shapes=[pltpu.VMEM((s[4], COLS), BF16) for s in steps]
        + [pltpu.VMEM(terms[i][1], F32) for i in picked]
        + [pltpu.SemaphoreType.DMA] * (n_steps + len(picked)),
        compiler_params=pltpu.CompilerParams(vmem_limit_bytes=24 * 2**20),
        cost_estimate=pl.CostEstimate(flops=cost*100, bytes_accessed=cost, transcendentals=0),
        name=name,
    )(parts, *[t[0] if i in picked else hold(t) for i, t in enumerate(terms)], *after)


def encode(mom, vert, horiz):
    rows = mom.shape[0]
    w_high, w_low = split(horiz)
    x_high, x_low = split(mom)
    out = []
    for b in range(NB):
        cut = slice(b * GROUP, (b + 1) * GROUP)
        half = dot(x_high[:, cut], w_high) + dot(x_low[:, cut], w_high) + dot(x_high[:, cut], w_low)
        out.append(jnp.sum(half.reshape(rows // GROUP, GROUP, BAND) * vert[None], axis=1))
    return out


def step_rows(grad_parts, momentum, params, vert, horiz):
    parts = pltpu.with_memory_space_constraint(grad_parts.reshape(4, 2, 2, OWN, COLS), pltpu.HBM)
    vert_t, horiz_t = vert.T, horiz.T
    zr, yr, half = ZROWS, OWN - ZROWS, COLS // 2
    left, right = slice(0, half), slice(half, COLS)
    call = lambda name, *rest, **options: piece_call(name, parts, *rest, **options)
    up, down = (lambda v: swap(v, z=1)), (lambda v: swap(v, z=3))
    OPP, UP, DOWN, MINE = 2, 1, 3, 0

    def z_rows(f, r, c):
        return (f, r, c, 0, zr)

    def y_rows(f, r, c):
        return (f, r, c, zr, yr)

    def widen(name, groups, after, more=None):
        extra = 0 if more is None else more.shape[0]
        outs, first = [], 0
        for group in groups:
            tail = extra if group is groups[-1] else 0

            def body(z, piece, term, out, group=group, first=first, tail=tail):
                top = 0
                for i, step in enumerate(group):
                    out[top:top + step[4], :] = piece(first + i)[...].astype(F32)
                    top += step[4]
                if tail:
                    out[top:, :] = term(0)[...]

            outs.append(((sum(s[4] for s in group) + tail, COLS), body))
            first += len(group)
        return call(name, [s for group in groups for s in group], [] if more is None else [more], after, outs)

    def add(i_pieces, i_term, first, cols=slice(None), half_terms=(), full_terms=()):
        def run(z, piece, term, out):
            top = 0
            for i in i_pieces:
                n = piece(i).shape[0]
                cut = slice(top, top + n)
                value = term(i_term)[first + top:first + top + n, cols] + piece(i)[:, cols].astype(F32)
                for k in full_terms:
                    value = value + term(k)[cut, cols]
                for k in half_terms:
                    value = value + term(k)[cut]
                out[cut, :] = value
                top += n
        return run

    def side(i_pieces, i_term, first, h_add, i_add):
        def run(z, piece, term, out):
            for h, cols in enumerate((left, right)):
                body = add(i_pieces, i_term, first, cols, (i_add,) if h == h_add else ())
                body(z, piece, term, out.at[:, cols])
        return run

    w_first, ta = widen("widen_a", [[z_rows(OPP, 0, 1), z_rows(OPP, 1, 1), y_rows(OPP, 1, 1)]], [])
    c_first = swap(w_first, core=1)
    *w_b, tb = widen("widen_b", [
        [z_rows(UP, 0, 1), z_rows(UP, 1, 1)], [z_rows(DOWN, 0, 1), z_rows(DOWN, 1, 1)],
        [y_rows(UP, 1, 1), y_rows(DOWN, 1, 1), y_rows(MINE, 1, 1), y_rows(OPP, 0, 1)],
        [z_rows(MINE, 0, 1), z_rows(MINE, 1, 1)],
        [y_rows(UP, 0, 1), y_rows(DOWN, 0, 1), y_rows(MINE, 0, 1)]], [ta], params)
    c_up, c_down, c_cross, c_own, c_rest = [swap(w, core=1) for w in w_b]
    def params_part(top, n):
        def pick(x, ref):
            return ref.at[pl.ds(pl.multiple_of((x % 2) * (OWN // 2) + top, FIRST), n), :]
        return (params, (n, COLS), pick)

    def with_params(body, i_params):
        def run(z, piece, term, out):
            n = out.shape[0] - term(i_params).shape[0]
            body(z, piece, term, out.at[:n])
            out[n:, :] = term(i_params)[...]
        return run

    u1, d1, y1, t1 = call(
        "opposite", [z_rows(OPP, 0, 0), z_rows(OPP, 1, 0), y_rows(OPP, 1, 0)], [c_first, params_part(0, FIRST)], [tb],
        [((2 * zr, half), add((0, 1), 0, 0, left)), ((2 * zr, half), add((0, 1), 0, 0, right)),
         ((yr + FIRST, COLS), with_params(add((2,), 0, 2 * zr), 1))])
    gu1, gd1, gy1 = up(u1), down(d1), swap(y1, y=2)

    table_high, table_low, tt = call("band_table", [], [vert_t, horiz_t], [t1], band_table())
    fold = yr // 2

    def onward(i, first, h_add, i_add, cols):
        def run(z, piece, term, out):
            side((2 * i, 2 * i + 1), i, 0, h_add, i_add)(z, piece, term, out.at[:2 * zr])
            value = term(4)[3 * yr:, cols] + term(5)[:yr, cols] + piece(4)[:, cols].astype(F32)
            out[2 * zr:, left] = value[:fold]
            out[2 * zr:, right] = value[fold:]
        return run

    y2, _ = call(
        "crossing", [y_rows(UP, 1, 0), y_rows(DOWN, 1, 0), y_rows(MINE, 1, 0)],
        [c_cross, params_part(FIRST, OWN // 2 - FIRST)], [t1],
        [((3 * yr + OWN // 2 - FIRST, COLS), with_params(add((0, 1, 2), 0, 0), 1))])
    u2, d2, t2 = call(
        "sides", [z_rows(UP, 0, 0), z_rows(UP, 1, 0), z_rows(DOWN, 0, 0), z_rows(DOWN, 1, 0), y_rows(OPP, 0, 0)],
        [c_up, c_down, gu1, gd1, c_cross, gy1], [tt],
        [((2 * zr + fold, COLS), onward(0, 0, 0, 2, left)), ((2 * zr + fold, COLS), onward(1, 0, 1, 3, right))], cost=100000000)
    gu2, gd2, gy2 = up(u2), down(d2), swap(y2, y=2)

    def own_body(r):
        def run(z, piece, term, out):
            cut = slice(r * zr, (r + 1) * zr)
            out[...] = term(0)[cut] + piece(r)[...].astype(F32) + (term(1)[cut] + term(2)[cut])
        return run

    def last_side(i, h_add, i_add):
        def run(z, piece, term, out):
            cut = slice(i * yr, (i + 1) * yr)
            for h, cols in enumerate((left, right)):
                value = term(3)[cut, cols] + term(4)[cut, cols] + piece(2 + i)[:, cols].astype(F32)
                if h == h_add:
                    out[:fold, cols] = value[:fold] + term(i_add)[2 * zr:, left]
                    out[fold:, cols] = value[fold:] + term(i_add)[2 * zr:, right]
                else:
                    out[:, cols] = value
        return run

    def last_own_body(z, piece, term, out):
        out[...] = term(3)[2 * yr:3 * yr] + term(4)[2 * yr:3 * yr] + piece(4)[...].astype(F32)

    def far_body(z, piece, term, out):
        out[:FIRST, :] = term(0)[yr:, :]
        out[FIRST:, :] = term(1)[3 * yr:, :]

    far_half, tf = call("far_rows", [], [gy1, gy2], [t2], [((OWN // 2, COLS), far_body)], cost=1)
    far_rows, u4, d4, near, last_own, t6 = call(
        "own", [z_rows(MINE, 0, 0), z_rows(MINE, 1, 0), y_rows(UP, 0, 0), y_rows(DOWN, 0, 0), y_rows(MINE, 0, 0)],
        [c_own, gu2, gd2, gy2, c_rest], [tf],
        [((zr, COLS), own_body(1)), ((yr, COLS), last_side(0, 0, 1)), ((yr, COLS), last_side(1, 1, 2)),
         ((zr, COLS), own_body(0)), ((yr, COLS), last_own_body)])
    far_other = swap(far_half, x=1)
    from_core = [swap(far_half, core=1)]
    gu4, gd4 = up(u4), down(d4)
    def momentum_rows(top, n):
        return (momentum, (n, COLS), lambda x, ref: ref.at[pl.ds(top, n), :])

    nz, ny = zr // GROUP, yr // GROUP

    def near_partial(z, piece, term, out):
        value = beta * term(2)[...] + term(0)[...] * (1.0 / 16.0)
        for b, (mine, theirs) in enumerate(zip(encode(value, term(3)[...], term(4)[...]),
                                               encode(term(1)[...] * (1.0 / 16.0), term(3)[...], term(4)[...]))):
            out[b, :nz, :] = mine
            out[b, nz:, :] = theirs

    def hand_on(z, piece, term, out):
        out[...] = term(1)[...]

    partial, y3, _ = call("partial_encode", [], [near, far_rows, momentum_rows(0, zr), vert, horiz], [t6],
                        [((NB, 2 * nz, BAND), near_partial), ((zr, COLS), hand_on)])
    gy3 = swap(y3, y=2)

    def last_mom(z, piece, term, out):
        grad = term(0)[...] + (term(1)[...] + term(2)[...])
        out[...] = beta * term(3)[...] + grad * (1.0 / 16.0)
        last_mom.value = out

    def last_coeffs(z, piece, term, out):
        for b, value in enumerate(encode(last_mom.value[...], term(4)[...], term(5)[...])):
            out[b, :nz, :] = term(6)[b, :nz]
            out[b, nz:nz + ny, :] = value
            out[b, nz + ny:, :] = term(6)[b, nz:]

    mom_low, coeffs, t7 = call(
        "last_momentum", [], [last_own, gu4, gd4, momentum_rows(zr, yr), vert, horiz, partial], [t6, far_other, from_core[0]],
        [((yr, COLS), last_mom), ((NB, 2 * nz + ny, BAND), last_coeffs)], cost=4 * 10**6,
    )

    def sum_four(z, piece, term, out):
        out[...] = (term(0)[...] + term(2)[...]) + (term(1)[...] + term(3)[...])

    total, tx = call("sum_x", [], [coeffs] + [swap(coeffs, x=k) for k in (2, 1, 3)], [], [(coeffs.shape, sum_four)],
                    cost=20000000)
    def near_mom(z, piece, term, out):
        out[...] = beta * term(2)[...] + (term(0)[...] + term(1)[...]) * (1.0 / 16.0)
        near_mom.value = out

    def near_shared(z, piece, term, out):
        for b, value in enumerate(encode(near_mom.value[...], term(3)[...], term(4)[...])):
            out[b, :nz, :] = value
            out[b, nz:, :] = term(5)[b, nz:nz + ny]

    def far_copy(z, piece, term, out):
        out[...] = term(6)[...]

    mom_top, shared, far_late, t8 = call(
        "near_momentum", [], [near, gy3, momentum_rows(0, zr), vert, horiz, coeffs, far_other], [tx],
        [((zr, COLS), near_mom), ((NB, nz + ny, BAND), near_shared), ((OWN // 2, COLS), far_copy)], cost=5 * 10**6,
    )
    from_core.append(swap(far_late, core=1))

    def residual(z, piece, term, out):
        high, low = split(term(4)[...])
        w_both = jnp.concatenate([high, low], axis=1)
        vert_now = term(3)[...][None]
        for pair in range(NB // 2):
            sides = []
            for b in (2 * pair, 2 * pair + 1):
                wide = (term(2)[b][:, None, :] * vert_now).reshape(OWN, BAND)
                wide_high, wide_low = split(wide)
                both = dot(wide_high, w_both)
                sides.append(both[:, :GROUP] + both[:, GROUP:] + dot(wide_low, w_both[:, :GROUP]))
            cols = slice(pair * 2 * GROUP, (pair + 1) * 2 * GROUP)
            value = jnp.concatenate(sides, axis=1)
            out[:zr, cols] = term(0)[:, cols] - value[:zr]
            out[zr:, cols] = term(1)[:, cols] - value[zr:]

    new_momentum, t9 = call("momentum_residual", [], [mom_top, mom_low, shared, vert, horiz_t], [t8],
                            [((OWN, COLS), residual)], cost=9 * 10**6, result=True)

    def sum_pairs(z, piece, term, out):
        top, low, far = slice(0, nz), slice(nz, nz + ny), slice(nz + ny, None)
        for k, (a, b, c, d) in enumerate(((0, 2, 1, 3), (1, 3, 0, 2))):
            own = [term(a)[:, cut] + term(b)[:, cut] for cut in (top, low)]
            out[k, :, :nz, :] = own[0] + (term(c)[:, far] + term(d)[:, far])
            out[k, :, nz:, :] = own[1]

    pair, _ = call("sum_y", [], [total] + [swap(total, y=k) for k in (2, 1, 3)], [t9], [((2,) + shared.shape, sum_pairs)],
                   cost=7 * 10**7)
    new_params = update_call([params, far_half, far_other, c_rest] + from_core, pair, swap(pair, core=1), table_high, table_low)
    return new_momentum, new_params


def band_table():
    held = {}

    def high(z, piece, term, out):
        lane = lax.broadcasted_iota(jnp.int32, (BAND, 2 * GROUP), 1)
        horiz = jnp.concatenate([term(1)[...]] * 2, axis=1)
        vert = term(0)[...]
        held["low"] = []
        for m in range(0, GROUP, 2):
            product = jnp.where(lane < GROUP, vert[:, m:m + 1], vert[:, m + 1:m + 2]) * horiz
            top, rest = split(product)
            out[:, m * GROUP:(m + 2) * GROUP] = top
            held["low"].append(rest)

    def low(z, piece, term, out):
        for i, rest in enumerate(held["low"]):
            out[:, 2 * i * GROUP:2 * (i + 1) * GROUP] = rest

    return [((BAND, GROUP * GROUP), high, BF16), ((BAND, GROUP * GROUP), low, BF16)]


def update_kernel(own_ref, far_ref, other_ref, core_own_ref, core_far_ref, core_other_ref,
                  pair_ref, pair_core_ref, high_ref, low_ref, out_ref, coeff, field, sems):
    dp = lax.axis_index("dp")
    odd = (lax.axis_index("outer") // 2) % 2
    nblock = OWN // GROUP
    part = nblock // 2
    core_own = core_own_ref.at[core_own_ref.shape[0] - nblock:]
    rows = ((own_ref,), (core_own,), (far_ref, other_ref), (core_far_ref, core_other_ref))
    for k in range(4):
        value = (pair_ref, pair_core_ref)[k % 2][k // 2]
        if k >= 2:
            turned = jnp.concatenate([value[:, part:], value[:, :part]], axis=1)
            value = jnp.where(odd == 1, turned, value)
        coeff[:, k] = value
    c_high, c_low = split(coeff[...].reshape(NB * 4 * nblock, BAND) * (1.0 / 8.0))
    both = jnp.concatenate([c_high, c_low], axis=0)
    lane = lax.broadcasted_iota(jnp.int32, (4 * nblock, 2 * GROUP), 1)
    first = lane < GROUP
    step = 8
    stores = []
    for c in range(GROUP // step):
        cols = slice(c * step * GROUP, (c + 1) * step * GROUP)
        wide = dot(both, high_ref[:, cols])
        value = wide[:NB * 4 * nblock] + wide[NB * 4 * nblock:] + dot(c_high, low_ref[:, cols])
        at = slice(c * step, (c + 1) * step)
        for b in range(0, NB, 2):
            x0, x1 = [value[i * 4 * nblock:(i + 1) * 4 * nblock] for i in (b, b + 1)]
            rows_m = []
            for lt in range(step // 2):
                lanes = slice(lt * 2 * GROUP, (lt + 1) * 2 * GROUP)
                y0, y1 = x0[:, lanes], x1[:, lanes]
                rows_m.append(jnp.where(first, y0, pltpu.roll(y1, GROUP, 1)))
                rows_m.append(jnp.where(first, pltpu.roll(y0, GROUP, 1), y1))
            turned = jnp.swapaxes(jnp.stack(rows_m), 0, 1)
            out_cols = slice(b * GROUP, (b + 2) * GROUP)
            for k in range(4):
                n = nblock // len(rows[k])
                for i, ref in enumerate(rows[k]):
                    to = pl.ds(part * ((odd + i) % 2), part) if k >= 2 else slice(None)
                    field[k, to, at, out_cols] = ref[:, at, out_cols] - turned[k * nblock + i * n:k * nblock + (i + 1) * n]
        for k in range(4):
            store = pltpu.make_async_copy(field.at[k, :, pl.ds(c * step, step), :],
                                          out_ref.at[dp ^ k, :, pl.ds(c * step, step), :], sems.at[c * 4 + k])
            store.start()
            stores.append(store)
    for store in stores:
        store.wait()


def update_call(rows, *arrays):
    arrays = [r.reshape(-1, GROUP, COLS) for r in rows] + list(arrays)
    return pl.pallas_call(
        update_kernel,
        in_specs=[pl.BlockSpec(memory_space=pltpu.VMEM)] * len(arrays),
        out_specs=pl.BlockSpec(memory_space=pl.ANY),
        out_shape=jax.ShapeDtypeStruct((4, OWN // GROUP, GROUP, COLS), F32),
        scratch_shapes=[
            pltpu.VMEM((NB, 4, OWN // GROUP, BAND), F32),
            pltpu.VMEM((4, OWN // GROUP, GROUP, COLS), F32),
            pltpu.SemaphoreType.DMA((4 * GROUP // 8,)),
        ],
        compiler_params=pltpu.CompilerParams(vmem_limit_bytes=24 * 2**20),
        name="parameter_update",
    )(*[pltpu.with_memory_space_constraint(a, pltpu.VMEM) for a in arrays]).reshape(4 * OWN, COLS)


def local(grad_parts, momentum, params, band):
    band = band.astype(jnp.int32)
    vert = cosine_columns(band // GROUP)
    horiz = cosine_columns(band % GROUP)
    new_momentum, new_params = step_rows(grad_parts, momentum[0], params, vert, horiz)
    return (new_momentum[None], new_params)


def solution(mesh):
    return jax.shard_map(
        local,
        mesh=mesh,
        in_specs=(
            P("outer", "fsdp", "dp", None, None),
            P("outer", ("fsdp", "dp"), None),
            P(("fsdp", "dp"), None),
            P(),
        ),
        out_specs=(P("outer", ("fsdp", "dp"), None), P("fsdp", None)),
        check_vma=False,
    )
```
